256 devices in a mesh: layer: 4 (over y), tile: 64 (over z, x, core).
Axes of the slice: x: 4, y: 4, z: 8, core: 2. Of those that a mesh axis runs over, the one named last changes fastest.
Arguments:
- source_field: float32 [16, 2, 16, 64, 512], P('layer', None, None, 'tile'), may hold values from -4 to 4
- wave_shift: float32 [16, 2, 64, 512], P('layer', None, 'tile'), may hold values from 0.2 to 2
- frontal_blocks: bfloat16 [4, 256, 8, 2, 128, 128], P('layer', 'tile'), may hold values from -0.125 to 0.125
- block_columns: int32 [4, 256, 8], P('layer', 'tile'), may hold values from 0 to 8
Outputs:
- solution_field: float32 [16, 2, 16, 64, 512], P('layer', None, None, 'tile')
- residual_field: float32 [16, 2, 16, 64, 512], P('layer', None, None, 'tile')
The draws below stay inside these ranges and needn't reach their ends.
Inputs may be any that keep to these rules, and one draw needn't show every extreme that they name: `block_columns`: a value c in block row b refers to block b + c - 4; where that lies outside the plane the block adds nothing.
All inputs are finite; a program needn't handle non-finite values.
Results may differ from the reference program's by a relative error of at most 0.022.
Values may be sent and summed in bfloat16 or wider, within the bound.
A program may use at most 64 MiB of HBM per device.

```python
import jax
import jax.numpy as jnp
from jax import lax

BLK = 128
K = 8
REACH = 4
PL = 4
NZ = 512
RHS = 16
NB = 256
NY = 64
PLANES = 16
LAYERS = 4
N_LAYER = 4


def set_ends(entries, rng, least, high):
    spot = [jax.random.randint(jax.random.fold_in(rng, axis), (), 0, length) for axis, length in enumerate(entries.shape)]
    longest = entries.shape.index(max(entries.shape))
    neighbour = spot[:longest] + [(spot[longest] + 1) % entries.shape[longest]] + spot[longest + 1:]
    return entries.at[tuple(spot)].set(least).at[tuple(neighbour)].set(high)


def level_of(own_key, dims, shards, smallest, high):
    def one(position, blocks):
        draws = jax.random.uniform(jax.random.fold_in(jax.random.fold_in(own_key, 6), position), (blocks,), jnp.float32, smallest / len(shards), high / len(shards))
        return jnp.repeat(jnp.exp(draws), dims[position] // blocks).reshape((-1,) + (1,) * (len(dims) - position - 1))

    gain = one(*shards[0])
    for cut in shards[1:]:
        gain = gain * one(*cut)
    return gain


def noise(own_key, extent, deviation, limit, shards=(), kind=jnp.bfloat16):
    array = jax.random.normal(own_key, extent, jnp.float32) * deviation
    if len(shards) > 0:
        array = level_of(own_key, extent, shards, -0.22, 0.18) * array
    return jnp.clip(array, min=-limit, max=limit).astype(kind)


def setup_inputs(seed: int = 0) -> dict:
    keys = jax.random.split(jax.random.key(seed), 5)
    source_field = noise(keys[0], (PLANES, 2, RHS, NY, NZ), 0.5, 4.0, ((0, 4), (3, 64)), jnp.float32)
    wave_shift = jnp.clip(0.2 + 1.8 * jax.random.uniform(keys[1], (PLANES, 2, NY, NZ), jnp.float32) ** level_of(keys[1], (PLANES, 2, NY, NZ), ((0, 4), (2, 64)), -0.2, 0.2), 0.2, 2.0)
    frontal_blocks = noise(keys[2], (LAYERS, NB, K, 2, BLK, BLK), (2 * K * BLK) ** -0.5, 0.125, ((0, 4), (1, 64)))
    block_columns = set_ends(jax.random.randint(keys[3], (LAYERS, NB, K), 0, 2 * REACH + 1), jax.random.fold_in(keys[3], 1), 0, 2 * REACH).astype(jnp.int32)
    return {"source_field": source_field, "wave_shift": wave_shift, "frontal_blocks": frontal_blocks, "block_columns": block_columns}


def apply_front(vector, frontal, columns):
    count = frontal.shape[0]
    block_size = frontal.shape[-1]
    width_cols = vector.shape[1]
    rounded = lax.optimization_barrier(vector.astype(jnp.bfloat16))
    blocks = rounded.astype(jnp.float32).reshape(2, width_cols, count, block_size)
    padded = jnp.pad(blocks, ((0, 0), (0, 0), (REACH, REACH), (0, 0)))
    where_from = (jnp.arange(count, dtype=jnp.int32)[:, None] + columns).astype(jnp.int32)
    picked = padded[:, :, where_from]
    matrices = frontal.astype(jnp.float32)
    pattern = "rbkj,bkji->rbi"
    real_re = jnp.einsum(pattern, picked[0], matrices[:, :, 0])
    imag_im = jnp.einsum(pattern, picked[1], matrices[:, :, 1])
    real_im = jnp.einsum(pattern, picked[0], matrices[:, :, 1])
    imag_re = jnp.einsum(pattern, picked[1], matrices[:, :, 0])
    result = jnp.stack([real_re - imag_im, real_im + imag_re])
    return result.reshape(vector.shape)


def apply_operator(solution, wave_shift):
    padded = jnp.pad(solution, ((1, 1), (0, 0), (0, 0), (1, 1), (1, 1)))
    center = padded[1:-1, :, :, 1:-1, 1:-1]
    beside = padded[2:, :, :, 1:-1, 1:-1] + padded[:-2, :, :, 1:-1, 1:-1]
    beside = beside + padded[1:-1, :, :, 2:, 1:-1] + padded[1:-1, :, :, :-2, 1:-1]
    beside = beside + padded[1:-1, :, :, 1:-1, 2:] + padded[1:-1, :, :, 1:-1, :-2]
    shift_re = wave_shift[:, 0][:, None]
    shift_im = wave_shift[:, 1][:, None]
    value_re = (6.0 - shift_re) * center[:, 0] + shift_im * center[:, 1] - beside[:, 0]
    value_im = (6.0 - shift_re) * center[:, 1] - shift_im * center[:, 0] - beside[:, 1]
    return jnp.stack([value_re, value_im], axis=1)


def reference(source_field, wave_shift, frontal_blocks, block_columns):
    previous = jnp.zeros(source_field.shape[1:], jnp.float32)
    outputs = []
    for layer_index in range(N_LAYER):
        for plane_index in range(PL):
            place = layer_index * PL + plane_index
            previous = apply_front(source_field[place] + previous, frontal_blocks[layer_index], block_columns[layer_index])
            outputs.append(previous)
    solution = jnp.stack(outputs)
    residual = source_field - apply_operator(solution, wave_shift)
    return solution, residual
```

```python
import functools

import jax
import jax.numpy as jnp
from jax import lax
from jax.experimental import pallas as pl
from jax.experimental.pallas import tpu as pltpu
from jax.sharding import PartitionSpec as P

MESH = pl.DeviceIdType.MESH
F32, BF16 = jnp.float32, jnp.bfloat16
NB = 4
REMOTE = 5 * 128


def kernel(
    layers, tiles, src, shift, fro, col, sol, res,
    s_v, sh_v, fro_v, dense, ext, xo, xh, xlay, xs, acc, sol_v, res_v,
    lsem, lsend, lrecv, xsend, xrecv, csend, crecv, osem,
):
    l, t = lax.axis_index("layer"), lax.axis_index("tile")
    first, last = l == 0, l == layers - 1
    has_left, has_right = t > 0, t < tiles - 1

    barrier = pltpu.get_barrier_semaphore()
    for dl in (0, -1, 1):
        for dt in (-1, 0, 1):
            if dl == 0 and dt == 0:
                continue
            there = (l + dl >= 0) & (l + dl < layers) & (t + dt >= 0) & (t + dt < tiles)

            @pl.when(there)
            def _():
                pl.semaphore_signal(barrier, inc=1, device_id=(l + dl, t + dt), device_id_type=MESH)

    load_s = pltpu.make_async_copy(src, s_v.at[pl.ds(0, 4)], lsem.at[0])
    load_f = pltpu.make_async_copy(fro, fro_v, lsem.at[1])
    load_w = pltpu.make_async_copy(shift, sh_v, lsem.at[2])
    load_s.start()
    load_f.start()
    load_w.start()

    @pl.when(jnp.logical_not(has_left))
    def _():
        ext[:, 0:4] = jnp.zeros((5, 4, 32, 128), BF16)
        xh[:, 0] = jnp.zeros((4, 4, 32, 128), BF16)

    @pl.when(jnp.logical_not(has_right))
    def _():
        ext[:, 8:12] = jnp.zeros((5, 4, 32, 128), BF16)
        xh[:, 1] = jnp.zeros((4, 4, 32, 128), BF16)

    @pl.when(first)
    def _():
        xlay[0] = jnp.zeros((4, 32, 128), BF16)

    @pl.when(last)
    def _():
        xlay[1] = jnp.zeros((4, 32, 128), BF16)
        s_v[4] = jnp.zeros((2, 64, 128), F32)

    def source(q, part, b):
        return s_v[q, part, pl.ds(b, 16, stride=4), :]

    load_s.wait()

    @pl.when(first)
    def _():
        for b in range(NB):
            ext[0, 4 + b, 0:16] = source(0, 0, b).astype(BF16)
            ext[0, 4 + b, 16:32] = source(0, 1, b).astype(BF16)

    rows = jnp.where(first | last, 2, 3)
    cols = jnp.where(has_left & has_right, 3, 2)
    pl.semaphore_wait(barrier, rows * cols - 1)

    def load_copy(q, dt, to):
        return pltpu.make_async_remote_copy(
            src_ref=ext.at[q, pl.ds(4, 4)],
            dst_ref=ext.at[lax.rem(q, 4), pl.ds(4 - 4 * dt, 4)],
            send_sem=lsend.at[q, 1 + dt],
            recv_sem=lrecv.at[lax.rem(q, 4), 1 - dt],
            device_id=(to, t + dt),
            device_id_type=MESH,
        )

    def x_copy(q, dt):
        side = (1 - dt) // 2
        return pltpu.make_async_remote_copy(
            src_ref=xo.at[q],
            dst_ref=xh.at[q, side],
            send_sem=xsend.at[q, side],
            recv_sem=xrecv.at[q, side],
            device_id=(l, t + dt),
            device_id_type=MESH,
        )

    def layer_copy(dl):
        side = (1 - dl) // 2
        return pltpu.make_async_remote_copy(
            src_ref=xo.at[3 if dl == 1 else 0],
            dst_ref=xlay.at[side],
            send_sem=csend.at[side],
            recv_sem=crecv.at[side],
            device_id=(l + dl, t),
            device_id_type=MESH,
        )

    def source_copy():
        return pltpu.make_async_remote_copy(
            src_ref=s_v.at[0],
            dst_ref=s_v.at[4],
            send_sem=csend.at[2],
            recv_sem=crecv.at[2],
            device_id=(l - 1, t),
            device_id_type=MESH,
        )

    @pl.when(first & has_left)
    def _():
        load_copy(0, -1, l).start()

    @pl.when(first & has_right)
    def _():
        load_copy(0, 1, l).start()

    @pl.when(jnp.logical_not(first))
    def _():
        source_copy().start()

    load_f.wait()

    def densify(i, carry):
        b, r = i // 8, lax.rem(i, 8) * 16
        hit = [[col[b, k] == o for k in range(8)] for o in range(9)]
        for part in range(2):
            blocks = [fro_v[b, k, part, pl.ds(r, 16), :].astype(F32) for k in range(8)]
            for o in range(9):
                place = jnp.where(o < 4 - b, o, jnp.where(o >= 8 - b, o - 4, o + 1 + b))
                total = jnp.zeros((16, 128), F32)
                for k in range(8):
                    total = total + jnp.where(hit[o][k], blocks[k], 0.0)
                dense[b, pl.ds(pl.multiple_of(place * 128 + r, 16), 16), part * 128 : part * 128 + 128] = total.astype(BF16)
        return carry

    lax.fori_loop(0, 32, densify, 0)

    def plane(q, carry):
        @pl.when(jnp.logical_not(first) & (q == 0))
        def _():
            load_copy(0, 0, l).wait_recv()

        own = jnp.concatenate([ext[q, 4 + c] for c in range(4)], axis=1)
        for b in range(NB):
            acc[b] = jnp.dot(own, dense[b, REMOTE:], preferred_element_type=F32)

        @pl.when((q == 3) & jnp.logical_not(last))
        def _():
            source_copy().wait_recv()

        @pl.when(has_left)
        def _():
            load_copy(q, 1, l).wait_recv()

        @pl.when(has_right)
        def _():
            load_copy(q, -1, l).wait_recv()

        for b in range(NB):
            beside = [ext[q, c] for c in range(b, 4)] + [ext[q, 8 + c] for c in range(b + 1)]
            total = acc[b] + jnp.dot(
                jnp.concatenate(beside, axis=1), dense[b, 0:REMOTE], preferred_element_type=F32
            )
            re = total[0:16, 0:128] - total[16:32, 128:256]
            im = total[0:16, 128:256] + total[16:32, 0:128]
            ext[q + 1, 4 + b, 0:16] = (source(q + 1, 0, b) + re).astype(BF16)
            ext[q + 1, 4 + b, 16:32] = (source(q + 1, 1, b) + im).astype(BF16)
            xs[q + 1, 0, b] = re
            xs[q + 1, 1, b] = im

        onward = (q < 3) | jnp.logical_not(last)
        to = l + q // 3

        @pl.when(onward & has_left)
        def _():
            load_copy(q + 1, -1, to).start()

        @pl.when(onward & has_right)
        def _():
            load_copy(q + 1, 1, to).start()

        @pl.when((q == 3) & jnp.logical_not(last))
        def _():
            load_copy(q + 1, 0, to).start()

        for b in range(NB):
            for part in range(2):
                value = xs[q + 1, part, b]
                xo[q, b, part * 16 : part * 16 + 16] = value.astype(BF16)
                sol_v[q, part, pl.ds(b, 16, stride=4), :] = value

        @pl.when(has_left)
        def _():
            x_copy(q, -1).start()

        @pl.when(has_right)
        def _():
            x_copy(q, 1).start()

        @pl.when((q == 0) & jnp.logical_not(first))
        def _():
            layer_copy(-1).start()

        @pl.when((q == 3) & jnp.logical_not(last))
        def _():
            layer_copy(1).start()

        pltpu.make_async_copy(sol_v.at[q], sol.at[q], osem.at[0, q]).start()
        return carry

    lax.fori_loop(0, 4, plane, 0)

    load_w.wait()

    @pl.when(jnp.logical_not(first))
    def _():
        layer_copy(1).wait_recv()

    @pl.when(jnp.logical_not(last))
    def _():
        layer_copy(-1).wait_recv()

    for b in range(NB):
        for part in range(2):
            xs[0, part, b] = xlay[0, b, part * 16 : part * 16 + 16].astype(F32)
            xs[5, part, b] = xlay[1, b, part * 16 : part * 16 + 16].astype(F32)

    lane = lax.broadcasted_iota(jnp.int32, (16, 128), 1)

    def residual(q, carry):
        @pl.when(has_left)
        def _():
            x_copy(q, 1).wait_recv()

        @pl.when(has_right)
        def _():
            x_copy(q, -1).wait_recv()

        for b in range(NB):
            s_re = 6.0 - sh_v[q, pl.ds(b, 1), :]
            s_im = sh_v[q, pl.ds(4 + b, 1), :]
            x = [xs[q + 1, part, b] for part in range(2)]
            for part in range(2):
                up = pltpu.roll(x[part], 1, 1)
                before = pltpu.roll(xs[q + 1, part, b - 1], 1, 1) if b > 0 else jnp.zeros_like(up)
                down = pltpu.roll(x[part], 127, 1)
                after = pltpu.roll(xs[q + 1, part, b + 1], 127, 1) if b < 3 else jnp.zeros_like(up)
                beside = jnp.where(lane == 0, before, up) + jnp.where(lane == 127, after, down)
                beside = beside + xs[q, part, b] + xs[q + 2, part, b]
                half = slice(part * 16, part * 16 + 16)
                beside = beside + xh[q, 0, b, half].astype(F32) + xh[q, 1, b, half].astype(F32)
                cross = s_im * x[1] if part == 0 else -(s_im * x[0])
                value = s_re * x[part] + cross - beside
                res_v[q, part, pl.ds(b, 16, stride=4), :] = source(q, part, b) - value
        pltpu.make_async_copy(res_v.at[q], res.at[q], osem.at[1, q]).start()
        return carry

    lax.fori_loop(0, 4, residual, 0)

    @pl.when(first & has_left)
    def _():
        load_copy(0, -1, l).wait_send()

    @pl.when(first & has_right)
    def _():
        load_copy(0, 1, l).wait_send()

    @pl.when(jnp.logical_not(first))
    def _():
        source_copy().wait_send()
        layer_copy(-1).wait_send()

    @pl.when(jnp.logical_not(last))
    def _():
        load_copy(4, 0, l).wait_send()
        layer_copy(1).wait_send()

    def drain(q, carry):
        onward = (q < 3) | jnp.logical_not(last)

        @pl.when(has_left)
        def _():
            x_copy(q, -1).wait_send()

        @pl.when(has_right)
        def _():
            x_copy(q, 1).wait_send()

        @pl.when(onward & has_left)
        def _():
            load_copy(q + 1, -1, l).wait_send()

        @pl.when(onward & has_right)
        def _():
            load_copy(q + 1, 1, l).wait_send()

        pltpu.make_async_copy(sol_v.at[q], sol.at[q], osem.at[0, q]).wait()
        pltpu.make_async_copy(res_v.at[q], res.at[q], osem.at[1, q]).wait()
        return carry

    lax.fori_loop(0, 4, drain, 0)


def per_device(layers, tiles, source_field, wave_shift, frontal_blocks, block_columns):
    field = jax.ShapeDtypeStruct((4, 2, 64, 128), F32)
    hbm = pl.BlockSpec(memory_space=pl.ANY)
    dma = pltpu.SemaphoreType.DMA
    sol, res = pl.pallas_call(
        functools.partial(kernel, layers, tiles),
        out_shape=(field, field),
        in_specs=[hbm, hbm, hbm, pl.BlockSpec(memory_space=pltpu.SMEM)],
        out_specs=(hbm, hbm),
        scratch_shapes=[
            pltpu.VMEM((5, 2, 64, 128), F32),
            pltpu.VMEM((4, 8, 128), F32),
            pltpu.VMEM((4, 8, 2, 128, 128), BF16),
            pltpu.VMEM((4, 1152, 256), BF16),
            pltpu.VMEM((5, 12, 32, 128), BF16),
            pltpu.VMEM((4, 4, 32, 128), BF16),
            pltpu.VMEM((4, 2, 4, 32, 128), BF16),
            pltpu.VMEM((2, 4, 32, 128), BF16),
            pltpu.VMEM((6, 2, 4, 16, 128), F32),
            pltpu.VMEM((4, 32, 256), F32),
            pltpu.VMEM((4, 2, 64, 128), F32),
            pltpu.VMEM((4, 2, 64, 128), F32),
            dma((3,)),
            dma((5, 3)),
            dma((4, 3)),
            dma((4, 2)),
            dma((4, 2)),
            dma((3,)),
            dma((3,)),
            dma((2, 4)),
        ],
        compiler_params=pltpu.CompilerParams(
            collective_id=0, has_side_effects=True, vmem_limit_bytes=32 * 1024 * 1024
        ),
    )(
        source_field.reshape(4, 2, 64, 128),
        wave_shift.reshape(4, 8, 128),
        frontal_blocks[0],
        block_columns[0],
    )
    return sol.reshape(4, 2, 16, 1, 512), res.reshape(4, 2, 16, 1, 512)


def solution(mesh):
    placed = (
        P("layer", None, None, "tile", None),
        P("layer", None, "tile", None),
        P("layer", "tile", None, None, None, None),
        P("layer", "tile", None),
    )
    return jax.shard_map(
        functools.partial(per_device, mesh.shape["layer"], mesh.shape["tile"]),
        mesh=mesh,
        in_specs=placed,
        out_specs=(P("layer", None, None, "tile", None), P("layer", None, None, "tile", None)),
        check_vma=False,
    )
```

```python
import functools

import jax
import jax.numpy as jnp
from jax import lax
from jax.experimental import pallas as pl
from jax.experimental.pallas import tpu as pltpu
from jax.sharding import PartitionSpec as P

MESH = pl.DeviceIdType.MESH
F32, BF16 = jnp.float32, jnp.bfloat16
NB = 4
TURN = 8
PAIRED = 2
FAR_LEFT, LEFT, OWN, RIGHT, FAR_RIGHT = 0, 4, 8, 12, 16
REMOTE = 5


def stages(b):
    return [
        ([3 - j] if 3 - j >= b else []) + ([8 + j] if j <= b else []) for j in range(4)
    ]


def places(b):
    return [c for stage in stages(b) for c in stage] + [4, 5, 6, 7]


def kernel(
    layers, tiles, src, shift, fro, columns, sol, res,
    s_v, sh_v, fro_v, col, dense, other, s_other, ext, xo, xh, xlay, xs, acc, sol_v, res_v,
    lsem, lsend, lrecv, fsend, frecv, xsend, xrecv, csend, crecv, gsend, grecv, osem,
):
    l, t = lax.axis_index("layer"), lax.axis_index("tile")
    first, last = l == 0, l == layers - 1
    has_left, has_right = t > 0, t < tiles - 1
    w = lax.rem(t, TURN)
    turn_left, turn_right = has_left & (w == 0), has_right & (w == TURN - 1)
    far_left = (t > 1) & (w <= 1)
    far_right = (t < tiles - 2) & (w >= TURN - 2)
    far = jnp.where(far_right, 2, -2)
    paired = l >= PAIRED

    barrier = pltpu.get_barrier_semaphore()
    for dl in (0, -1, 1):
        layer_there = (l + dl >= 0) & (l + dl < layers)
        for dt in (-1, 0, 1):
            if dl == 0 and dt == 0:
                continue
            there = layer_there & (t + dt >= 0) & (t + dt < tiles)

            @pl.when(there)
            def _():
                pl.semaphore_signal(barrier, inc=1, device_id=(l + dl, t + dt), device_id_type=MESH)

    for dl in (0, -1, 1):
        layer_there = (l + dl >= 0) & (l + dl < layers)

        @pl.when(layer_there & (far_left | far_right) & (l + max(dl, 0) >= PAIRED))
        def _():
            pl.semaphore_signal(barrier, inc=1, device_id=(l + dl, t + far), device_id_type=MESH)

    load_c = pltpu.make_async_copy(columns, col, lsem.at[0])
    load_s = pltpu.make_async_copy(src, s_v.at[pl.ds(0, 4)], lsem.at[1])
    load_w = pltpu.make_async_copy(shift, sh_v, lsem.at[2])
    load_f = [pltpu.make_async_copy(fro.at[b], fro_v.at[b], lsem.at[3 + b]) for b in range(NB)]
    load_c.start()
    load_f[0].start()
    load_s.start()
    for b in range(1, NB):
        load_f[b].start()
    load_w.start()

    @pl.when(jnp.logical_not(has_left))
    def _():
        ext[:, LEFT : LEFT + 4] = jnp.zeros((5, 4, 32, 128), BF16)
        xh[:, 0] = jnp.zeros((4, 4, 32, 128), BF16)

    @pl.when(jnp.logical_not(has_right))
    def _():
        ext[:, RIGHT : RIGHT + 4] = jnp.zeros((5, 4, 32, 128), BF16)
        xh[:, 1] = jnp.zeros((4, 4, 32, 128), BF16)

    @pl.when(first)
    def _():
        xlay[0] = jnp.zeros((4, 32, 128), BF16)

    @pl.when(last)
    def _():
        xlay[1] = jnp.zeros((4, 32, 128), BF16)
        s_v[4] = jnp.zeros((2, 64, 128), F32)

    def source(q, part, b):
        return s_v[q, part, pl.ds(b, 16, stride=4), :]

    load_c.wait()
    for b in range(NB):
        load_f[b].wait()
        hit = [[col[b, k] == c - b for k in range(8)] for c in places(b)]

        def densify(i, carry, b=b, hit=hit):
            r = pl.multiple_of(i * 16, 16)
            for part in range(2):
                blocks = [fro_v[b, k, part, pl.ds(r, 16), :].astype(F32) for k in range(8)]
                for place in range(9):
                    total = jnp.where(hit[place][0], blocks[0], 0.0)
                    for k in range(1, 8):
                        total = total + jnp.where(hit[place][k], blocks[k], 0.0)
                    dense[b, pl.ds(pl.multiple_of(place * 128 + r, 16), 16), part * 128 : part * 128 + 128] = total.astype(BF16)
            return carry

        lax.fori_loop(0, 8, densify, 0)

    load_s.wait()

    @pl.when(first)
    def _():
        for b in range(NB):
            ext[0, OWN + b, 0:16] = source(0, 0, b).astype(BF16)
            ext[0, OWN + b, 16:32] = source(0, 1, b).astype(BF16)

    rows = jnp.where(first | last, 2, 3)
    cols = jnp.where(has_left & has_right, 3, 2)
    far_rows = sum(
        jnp.where((l + dl >= 0) & (l + dl < layers) & (l + max(dl, 0) >= PAIRED), 1, 0) for dl in (0, -1, 1)
    )
    pl.semaphore_wait(barrier, rows * cols - 1 + jnp.where(far_left | far_right, far_rows, 0))

    def load_copy(q, dt, to, c):
        into = LEFT if dt == 1 else RIGHT
        return pltpu.make_async_remote_copy(
            src_ref=ext.at[q, OWN + c],
            dst_ref=ext.at[lax.rem(q, 4), into + c],
            send_sem=lsend.at[q, (1 + dt) // 2, c],
            recv_sem=lrecv.at[lax.rem(q, 4), (1 - dt) // 2, c],
            device_id=(to, t + dt),
            device_id_type=MESH,
        )

    def own_copy():
        return pltpu.make_async_remote_copy(
            src_ref=ext.at[4, pl.ds(OWN, 4)],
            dst_ref=ext.at[0, pl.ds(OWN, 4)],
            send_sem=csend.at[3],
            recv_sem=crecv.at[3],
            device_id=(l + 1, t),
            device_id_type=MESH,
        )

    def far_copy(q, dt, to):
        return pltpu.make_async_remote_copy(
            src_ref=ext.at[q, pl.ds(OWN, 4)],
            dst_ref=ext.at[lax.rem(q, 4), pl.ds(FAR_LEFT if dt == 2 else FAR_RIGHT, 4)],
            send_sem=fsend.at[q],
            recv_sem=frecv.at[lax.rem(q, 4)],
            device_id=(to, t + dt),
            device_id_type=MESH,
        )

    def x_copy(q, dt):
        side = (1 - dt) // 2
        return pltpu.make_async_remote_copy(
            src_ref=xo.at[q],
            dst_ref=xh.at[q, side],
            send_sem=xsend.at[q, side],
            recv_sem=xrecv.at[q, side],
            device_id=(l, t + dt),
            device_id_type=MESH,
        )

    def layer_copy(dl):
        side = (1 - dl) // 2
        return pltpu.make_async_remote_copy(
            src_ref=xo.at[3 if dl == 1 else 0],
            dst_ref=xlay.at[side],
            send_sem=csend.at[side],
            recv_sem=crecv.at[side],
            device_id=(l + dl, t),
            device_id_type=MESH,
        )

    def source_copy():
        return pltpu.make_async_remote_copy(
            src_ref=s_v.at[0],
            dst_ref=s_v.at[4],
            send_sem=csend.at[2],
            recv_sem=crecv.at[2],
            device_id=(l - 1, t),
            device_id_type=MESH,
        )

    across = t + jnp.where(turn_left, -1, 1)

    def turn_copies():
        pieces = [(dense, other), (s_v.at[1], s_other.at[0]), (s_v.at[3], s_other.at[1])]
        return [
            pltpu.make_async_remote_copy(
                src_ref=here,
                dst_ref=there,
                send_sem=gsend.at[i],
                recv_sem=grecv.at[i],
                device_id=(l, across),
                device_id_type=MESH,
            )
            for i, (here, there) in enumerate(pieces)
        ]

    at_turn = paired & (turn_left | turn_right)

    def sends_load(q, dt):
        there = has_left if dt == -1 else has_right
        turn = turn_left if dt == -1 else turn_right
        return there & jnp.logical_not(paired & turn & (lax.rem(q, 2) == 1))

    for step in range(4):
        @pl.when(first & has_left)
        def _():
            load_copy(0, -1, l, step).start()

        @pl.when(first & has_right)
        def _():
            load_copy(0, 1, l, 3 - step).start()

    @pl.when(jnp.logical_not(first))
    def _():
        source_copy().start()

    @pl.when(at_turn)
    def _():
        for copy in turn_copies()[::-1]:
            copy.start()

    def product(q, window, matrix, b, start, blocks):
        operand = jnp.concatenate([ext[q, window + c] for c in blocks], axis=1)
        return jnp.dot(
            operand,
            matrix[b, start * 128 : (start + len(blocks)) * 128],
            preferred_element_type=F32,
        )

    def combine(total):
        re = total[0:16, 0:128] - total[16:32, 128:256]
        im = total[0:16, 128:256] + total[16:32, 0:128]
        return re, im

    def plane(q, carry):
        @pl.when(jnp.logical_not(first) & (q == 0))
        def _():
            own_copy().wait_recv()

        for b in range(NB):
            acc[b] = product(q, LEFT, dense, b, REMOTE, [4, 5, 6, 7])

        @pl.when((q == 3) & jnp.logical_not(last))
        def _():
            source_copy().wait_recv()

        for j in range(4):
            @pl.when(sends_load(q, -1))
            def _():
                load_copy(q, 1, l, 3 - j).wait_recv()

            @pl.when(sends_load(q, 1))
            def _():
                load_copy(q, -1, l, j).wait_recv()

            for b in range(NB):
                needs = stages(b)[j]
                if not needs:
                    continue
                start = sum(len(s) for s in stages(b)[:j])
                total = acc[b] + product(q, LEFT, dense, b, start, needs)
                if any(stages(b)[j + 1 :]):
                    acc[b] = total
                    continue
                re, im = combine(total)
                ext[q + 1, OWN + b, 0:16] = (source(q + 1, 0, b) + re).astype(BF16)
                ext[q + 1, OWN + b, 16:32] = (source(q + 1, 1, b) + im).astype(BF16)
                xs[q + 1, 0, b] = re
                xs[q + 1, 1, b] = im

        handing = (q == 3) & jnp.logical_not(last)
        onward = (q < 3) | jnp.logical_not(last)
        to = l + q // 3

        for step in range(4):
            @pl.when(onward & (handing & has_left | (q < 3) & sends_load(q + 1, -1)))
            def _():
                load_copy(q + 1, -1, to, step).start()

            @pl.when(onward & (handing & has_right | (q < 3) & sends_load(q + 1, 1)))
            def _():
                load_copy(q + 1, 1, to, 3 - step).start()

        @pl.when(handing)
        def _():
            own_copy().start()

        sends_far = (handing & (l + 1 >= PAIRED)) | ((q == 1) & paired)

        @pl.when(sends_far & far_left & (w == 1))
        def _():
            far_copy(q + 1, -2, to).start()

        @pl.when(sends_far & far_right & (w == TURN - 2))
        def _():
            far_copy(q + 1, 2, to).start()

        @pl.when(at_turn & (lax.rem(q, 2) == 0))
        def _():
            @pl.when(q == 0)
            def _():
                for copy in turn_copies():
                    copy.wait_recv()

            window = jnp.where(turn_left, FAR_LEFT, OWN)
            into = jnp.where(turn_left, LEFT, RIGHT)
            for b in range(NB):
                acc[b] = product(q, window, other, b, REMOTE, [4, 5, 6, 7])

            @pl.when(turn_left)
            def _():
                far_copy(q, 2, l).wait_recv()

            @pl.when(turn_right)
            def _():
                far_copy(q, -2, l).wait_recv()

            for b in range(NB):
                total = acc[b] + product(q, window, other, b, 0, places(b)[:REMOTE])
                re, im = combine(total)
                there = [s_other[q // 2, part, pl.ds(b, 16, stride=4), :] for part in range(2)]
                ext[q + 1, into + b, 0:16] = (there[0] + re).astype(BF16)
                ext[q + 1, into + b, 16:32] = (there[1] + im).astype(BF16)

        for b in range(NB):
            for part in range(2):
                value = xs[q + 1, part, b]
                xo[q, b, part * 16 : part * 16 + 16] = value.astype(BF16)
                sol_v[q, part, pl.ds(b, 16, stride=4), :] = value

        @pl.when(has_left)
        def _():
            x_copy(q, -1).start()

        @pl.when(has_right)
        def _():
            x_copy(q, 1).start()

        @pl.when((q == 0) & jnp.logical_not(first))
        def _():
            layer_copy(-1).start()

        @pl.when(handing)
        def _():
            layer_copy(1).start()

        pltpu.make_async_copy(sol_v.at[q], sol.at[q], osem.at[0, q]).start()
        return carry

    lax.fori_loop(0, 4, plane, 0)

    load_w.wait()

    @pl.when(jnp.logical_not(first))
    def _():
        layer_copy(1).wait_recv()

    @pl.when(jnp.logical_not(last))
    def _():
        layer_copy(-1).wait_recv()

    for b in range(NB):
        for part in range(2):
            xs[0, part, b] = xlay[0, b, part * 16 : part * 16 + 16].astype(F32)
            xs[5, part, b] = xlay[1, b, part * 16 : part * 16 + 16].astype(F32)

    lane = lax.broadcasted_iota(jnp.int32, (16, 128), 1)

    def residual(q, carry):
        @pl.when(has_left)
        def _():
            x_copy(q, 1).wait_recv()

        @pl.when(has_right)
        def _():
            x_copy(q, -1).wait_recv()

        for b in range(NB):
            s_re = 6.0 - sh_v[q, pl.ds(b, 1), :]
            s_im = sh_v[q, pl.ds(4 + b, 1), :]
            x = [xs[q + 1, part, b] for part in range(2)]
            for part in range(2):
                up = pltpu.roll(x[part], 1, 1)
                before = pltpu.roll(xs[q + 1, part, b - 1], 1, 1) if b > 0 else jnp.zeros_like(up)
                down = pltpu.roll(x[part], 127, 1)
                after = pltpu.roll(xs[q + 1, part, b + 1], 127, 1) if b < 3 else jnp.zeros_like(up)
                beside = jnp.where(lane == 0, before, up) + jnp.where(lane == 127, after, down)
                beside = beside + xs[q, part, b] + xs[q + 2, part, b]
                half = slice(part * 16, part * 16 + 16)
                beside = beside + xh[q, 0, b, half].astype(F32) + xh[q, 1, b, half].astype(F32)
                cross = s_im * x[1] if part == 0 else -(s_im * x[0])
                value = s_re * x[part] + cross - beside
                res_v[q, part, pl.ds(b, 16, stride=4), :] = source(q, part, b) - value
        pltpu.make_async_copy(res_v.at[q], res.at[q], osem.at[1, q]).start()
        return carry

    lax.fori_loop(0, 4, residual, 0)

    for c in range(4):
        @pl.when(first & has_left)
        def _():
            load_copy(0, -1, l, c).wait_send()

        @pl.when(first & has_right)
        def _():
            load_copy(0, 1, l, c).wait_send()

    @pl.when(jnp.logical_not(first))
    def _():
        source_copy().wait_send()
        layer_copy(-1).wait_send()

    @pl.when(jnp.logical_not(last))
    def _():
        own_copy().wait_send()
        layer_copy(1).wait_send()

    @pl.when(at_turn)
    def _():
        for copy in turn_copies():
            copy.wait_send()

    @pl.when(paired & (far_left & (w == 1) | far_right & (w == TURN - 2)))
    def _():
        far_copy(2, 2, l).wait_send()

    @pl.when(jnp.logical_not(last) & (l + 1 >= PAIRED) & (far_left & (w == 1) | far_right & (w == TURN - 2)))
    def _():
        far_copy(4, 2, l).wait_send()

    def drain(q, carry):
        @pl.when(has_left)
        def _():
            x_copy(q, -1).wait_send()

        @pl.when(has_right)
        def _():
            x_copy(q, 1).wait_send()

        handing = (q == 3) & jnp.logical_not(last)
        for c in range(4):
            @pl.when(handing & has_left | (q < 3) & sends_load(q + 1, -1))
            def _():
                load_copy(q + 1, -1, l, c).wait_send()

            @pl.when(handing & has_right | (q < 3) & sends_load(q + 1, 1))
            def _():
                load_copy(q + 1, 1, l, c).wait_send()

        pltpu.make_async_copy(sol_v.at[q], sol.at[q], osem.at[0, q]).wait()
        pltpu.make_async_copy(res_v.at[q], res.at[q], osem.at[1, q]).wait()
        return carry

    lax.fori_loop(0, 4, drain, 0)


def per_device(layers, tiles, source_field, wave_shift, frontal_blocks, block_columns):
    field = jax.ShapeDtypeStruct((4, 2, 64, 128), F32)
    hbm = pl.BlockSpec(memory_space=pltpu.HBM)
    anywhere = pl.BlockSpec(memory_space=pl.ANY)
    dma = pltpu.SemaphoreType.DMA
    sol, res = pl.pallas_call(
        functools.partial(kernel, layers, tiles),
        out_shape=(field, field),
        in_specs=[hbm, hbm, hbm, hbm],
        out_specs=(anywhere, anywhere),
        scratch_shapes=[
            pltpu.VMEM((5, 2, 64, 128), F32),
            pltpu.VMEM((4, 8, 128), F32),
            pltpu.VMEM((4, 8, 2, 128, 128), BF16),
            pltpu.SMEM((4, 8), jnp.int32),
            pltpu.VMEM((4, 1152, 256), BF16),
            pltpu.VMEM((4, 1152, 256), BF16),
            pltpu.VMEM((2, 2, 64, 128), F32),
            pltpu.VMEM((5, 20, 32, 128), BF16),
            pltpu.VMEM((4, 4, 32, 128), BF16),
            pltpu.VMEM((4, 2, 4, 32, 128), BF16),
            pltpu.VMEM((2, 4, 32, 128), BF16),
            pltpu.VMEM((6, 2, 4, 16, 128), F32),
            pltpu.VMEM((4, 32, 256), F32),
            pltpu.VMEM((4, 2, 64, 128), F32),
            pltpu.VMEM((4, 2, 64, 128), F32),
            dma((7,)),
            dma((5, 2, 4)),
            dma((4, 2, 4)),
            dma((5,)),
            dma((4,)),
            dma((4, 2)),
            dma((4, 2)),
            dma((4,)),
            dma((4,)),
            dma((3,)),
            dma((3,)),
            dma((2, 4)),
        ],
        compiler_params=pltpu.CompilerParams(
            collective_id=0, has_side_effects=True, vmem_limit_bytes=60 * 1024 * 1024
        ),
    )(
        source_field.reshape(4, 2, 64, 128),
        wave_shift.reshape(4, 8, 128),
        frontal_blocks[0],
        block_columns[0],
    )
    return sol.reshape(4, 2, 16, 1, 512), res.reshape(4, 2, 16, 1, 512)


def solution(mesh):
    placed = (
        P("layer", None, None, "tile", None),
        P("layer", None, "tile", None),
        P("layer", "tile", None, None, None, None),
        P("layer", "tile", None),
    )
    return jax.shard_map(
        functools.partial(per_device, mesh.shape["layer"], mesh.shape["tile"]),
        mesh=mesh,
        in_specs=placed,
        out_specs=(P("layer", None, None, "tile", None), P("layer", None, None, "tile", None)),
        check_vma=False,
    )
```

```python
import functools

import jax
import jax.numpy as jnp
from jax import lax
from jax.experimental import pallas as pl
from jax.experimental.pallas import tpu as pltpu
from jax.sharding import PartitionSpec as P

MESH = pl.DeviceIdType.MESH
F32, BF16 = jnp.float32, jnp.bfloat16
NB = 4
TURN = 8
PAIRED = 2
FAR_LEFT, LEFT, OWN, RIGHT, FAR_RIGHT = 0, 4, 8, 12, 16
CUTS = 2
PIECE = NB // CUTS
REMOTE = 5


def stages(b):
    return [
        [c for c in range(4 - PIECE * (j + 1), 4 - PIECE * j) if c >= b]
        + [8 + c for c in range(PIECE * j, PIECE * (j + 1)) if c <= b]
        for j in range(CUTS)
    ]


def places(b):
    return [c for stage in stages(b) for c in stage] + [4, 5, 6, 7]


def kernel(
    layers, tiles, src, shift, fro, columns, sol, res,
    s_v, sh_v, fro_v, col, dense, other, s_other, ext, xo, xh, xlay, xs, acc, sol_v, res_v,
    lsem, lsend, lrecv, fsend, frecv, xsend, xrecv, csend, crecv, gsend, grecv, osem,
):
    l, t = lax.axis_index("layer"), lax.axis_index("tile")
    first, last = l == 0, l == layers - 1
    has_left, has_right = t > 0, t < tiles - 1
    w = lax.rem(t, TURN)
    turn_left, turn_right = has_left & (w == 0), has_right & (w == TURN - 1)
    far_left = (t > 1) & (w <= 1)
    far_right = (t < tiles - 2) & (w >= TURN - 2)
    far = jnp.where(far_right, 2, -2)
    paired = l >= PAIRED

    barrier = pltpu.get_barrier_semaphore()
    for dl in (0, -1, 1):
        layer_there = (l + dl >= 0) & (l + dl < layers)
        for dt in (-1, 0, 1):
            if dl == 0 and dt == 0:
                continue
            there = layer_there & (t + dt >= 0) & (t + dt < tiles)

            @pl.when(there)
            def _():
                pl.semaphore_signal(barrier, inc=1, device_id=(l + dl, t + dt), device_id_type=MESH)

    for dl in (0, -1, 1):
        layer_there = (l + dl >= 0) & (l + dl < layers)

        @pl.when(layer_there & (far_left | far_right) & (l + max(dl, 0) >= PAIRED))
        def _():
            pl.semaphore_signal(barrier, inc=1, device_id=(l + dl, t + far), device_id_type=MESH)

    load_c = pltpu.make_async_copy(columns, col, lsem.at[0])
    load_s = pltpu.make_async_copy(src, s_v.at[pl.ds(0, 4)], lsem.at[1])
    load_w = pltpu.make_async_copy(shift, sh_v, lsem.at[2])
    load_f = [pltpu.make_async_copy(fro.at[b], fro_v.at[b], lsem.at[3 + b]) for b in range(NB)]
    load_c.start()
    load_f[0].start()
    load_s.start()
    for b in range(1, NB):
        load_f[b].start()
    load_w.start()

    @pl.when(jnp.logical_not(has_left))
    def _():
        ext[:, LEFT : LEFT + 4] = jnp.zeros((5, 4, 32, 128), BF16)
        xh[:, 0] = jnp.zeros((4, 4, 32, 128), BF16)

    @pl.when(jnp.logical_not(has_right))
    def _():
        ext[:, RIGHT : RIGHT + 4] = jnp.zeros((5, 4, 32, 128), BF16)
        xh[:, 1] = jnp.zeros((4, 4, 32, 128), BF16)

    @pl.when(first)
    def _():
        xlay[0] = jnp.zeros((4, 32, 128), BF16)

    @pl.when(last)
    def _():
        xlay[1] = jnp.zeros((4, 32, 128), BF16)
        s_v[4] = jnp.zeros((2, 64, 128), F32)

    def source(q, part, b):
        return s_v[q, part, pl.ds(b, 16, stride=4), :]

    load_c.wait()
    for b in range(NB):
        load_f[b].wait()
        hit = [[col[b, k] == c - b for k in range(8)] for c in places(b)]

        def densify(i, carry, b=b, hit=hit):
            r = pl.multiple_of(i * 16, 16)
            for part in range(2):
                blocks = [fro_v[b, k, part, pl.ds(r, 16), :].astype(F32) for k in range(8)]
                for place in range(9):
                    total = jnp.where(hit[place][0], blocks[0], 0.0)
                    for k in range(1, 8):
                        total = total + jnp.where(hit[place][k], blocks[k], 0.0)
                    dense[b, pl.ds(pl.multiple_of(place * 128 + r, 16), 16), part * 128 : part * 128 + 128] = total.astype(BF16)
            return carry

        lax.fori_loop(0, 8, densify, 0)

    load_s.wait()

    @pl.when(first)
    def _():
        for b in range(NB):
            ext[0, OWN + b, 0:16] = source(0, 0, b).astype(BF16)
            ext[0, OWN + b, 16:32] = source(0, 1, b).astype(BF16)

    rows = jnp.where(first | last, 2, 3)
    cols = jnp.where(has_left & has_right, 3, 2)
    far_rows = sum(
        jnp.where((l + dl >= 0) & (l + dl < layers) & (l + max(dl, 0) >= PAIRED), 1, 0) for dl in (0, -1, 1)
    )
    pl.semaphore_wait(barrier, rows * cols - 1 + jnp.where(far_left | far_right, far_rows, 0))

    def load_copy(q, dt, to, j):
        into = LEFT if dt == 1 else RIGHT
        c = 4 - PIECE * (j + 1) if dt == 1 else PIECE * j
        return pltpu.make_async_remote_copy(
            src_ref=ext.at[q, pl.ds(OWN + c, PIECE)],
            dst_ref=ext.at[lax.rem(q, 4), pl.ds(into + c, PIECE)],
            send_sem=lsend.at[q, (1 + dt) // 2, j],
            recv_sem=lrecv.at[lax.rem(q, 4), (1 - dt) // 2, j],
            device_id=(to, t + dt),
            device_id_type=MESH,
        )

    def own_copy():
        return pltpu.make_async_remote_copy(
            src_ref=ext.at[4, pl.ds(OWN, 4)],
            dst_ref=ext.at[0, pl.ds(OWN, 4)],
            send_sem=csend.at[3],
            recv_sem=crecv.at[3],
            device_id=(l + 1, t),
            device_id_type=MESH,
        )

    def far_copy(q, dt, to):
        return pltpu.make_async_remote_copy(
            src_ref=ext.at[q, pl.ds(OWN, 4)],
            dst_ref=ext.at[lax.rem(q, 4), pl.ds(FAR_LEFT if dt == 2 else FAR_RIGHT, 4)],
            send_sem=fsend.at[q],
            recv_sem=frecv.at[lax.rem(q, 4)],
            device_id=(to, t + dt),
            device_id_type=MESH,
        )

    def x_copy(q, dt):
        side = (1 - dt) // 2
        return pltpu.make_async_remote_copy(
            src_ref=xo.at[q],
            dst_ref=xh.at[q, side],
            send_sem=xsend.at[q, side],
            recv_sem=xrecv.at[q, side],
            device_id=(l, t + dt),
            device_id_type=MESH,
        )

    def layer_copy(dl):
        side = (1 - dl) // 2
        return pltpu.make_async_remote_copy(
            src_ref=xo.at[3 if dl == 1 else 0],
            dst_ref=xlay.at[side],
            send_sem=csend.at[side],
            recv_sem=crecv.at[side],
            device_id=(l + dl, t),
            device_id_type=MESH,
        )

    def source_copy():
        return pltpu.make_async_remote_copy(
            src_ref=s_v.at[0],
            dst_ref=s_v.at[4],
            send_sem=csend.at[2],
            recv_sem=crecv.at[2],
            device_id=(l - 1, t),
            device_id_type=MESH,
        )

    across = t + jnp.where(turn_left, -1, 1)

    def turn_copies():
        pieces = [(dense, other), (s_v.at[1], s_other.at[0]), (s_v.at[3], s_other.at[1])]
        return [
            pltpu.make_async_remote_copy(
                src_ref=here,
                dst_ref=there,
                send_sem=gsend.at[i],
                recv_sem=grecv.at[i],
                device_id=(l, across),
                device_id_type=MESH,
            )
            for i, (here, there) in enumerate(pieces)
        ]

    at_turn = paired & (turn_left | turn_right)

    def sends_load(q, dt):
        there = has_left if dt == -1 else has_right
        turn = turn_left if dt == -1 else turn_right
        return there & jnp.logical_not(paired & turn & (lax.rem(q, 2) == 1))

    for step in range(CUTS):
        @pl.when(first & has_left)
        def _():
            load_copy(0, -1, l, step).start()

        @pl.when(first & has_right)
        def _():
            load_copy(0, 1, l, step).start()

    @pl.when(jnp.logical_not(first))
    def _():
        source_copy().start()

    @pl.when(at_turn)
    def _():
        for copy in turn_copies()[::-1]:
            copy.start()

    def product(q, window, matrix, b, start, blocks):
        operand = jnp.concatenate([ext[q, window + c] for c in blocks], axis=1)
        return jnp.dot(
            operand,
            matrix[b, start * 128 : (start + len(blocks)) * 128],
            preferred_element_type=F32,
        )

    def combine(total):
        re = total[0:16, 0:128] - total[16:32, 128:256]
        im = total[0:16, 128:256] + total[16:32, 0:128]
        return re, im

    def publish(q):
        for b in range(NB):
            for part in range(2):
                xo[q, b, part * 16 : part * 16 + 16] = xs[q + 1, part, b].astype(BF16)

        @pl.when(has_left)
        def _():
            x_copy(q, -1).start()

        @pl.when(has_right)
        def _():
            x_copy(q, 1).start()

        @pl.when((q == 0) & jnp.logical_not(first))
        def _():
            layer_copy(-1).start()

        @pl.when((q == 3) & jnp.logical_not(last))
        def _():
            layer_copy(1).start()

        for b in range(NB):
            for part in range(2):
                sol_v[q, part, pl.ds(b, 16, stride=4), :] = xs[q + 1, part, b]
        pltpu.make_async_copy(sol_v.at[q], sol.at[q], osem.at[0, q]).start()

    def plane(q, carry):
        @pl.when(jnp.logical_not(first) & (q == 0))
        def _():
            own_copy().wait_recv()

        for b in range(NB):
            acc[b] = product(q, LEFT, dense, b, REMOTE, [4, 5, 6, 7])

        @pl.when((q == 3) & jnp.logical_not(last))
        def _():
            source_copy().wait_recv()

        for j in range(CUTS):
            @pl.when(sends_load(q, -1))
            def _():
                load_copy(q, 1, l, j).wait_recv()

            @pl.when(sends_load(q, 1))
            def _():
                load_copy(q, -1, l, j).wait_recv()

            for b in range(NB):
                needs = stages(b)[j]
                if not needs:
                    continue
                start = sum(len(s) for s in stages(b)[:j])
                total = acc[b] + product(q, LEFT, dense, b, start, needs)
                if any(stages(b)[j + 1 :]):
                    acc[b] = total
                    continue
                re, im = combine(total)
                ext[q + 1, OWN + b, 0:16] = (source(q + 1, 0, b) + re).astype(BF16)
                ext[q + 1, OWN + b, 16:32] = (source(q + 1, 1, b) + im).astype(BF16)
                xs[q + 1, 0, b] = re
                xs[q + 1, 1, b] = im

        handing = (q == 3) & jnp.logical_not(last)
        onward = (q < 3) | jnp.logical_not(last)
        to = l + q // 3

        for step in range(CUTS):
            @pl.when(onward & (handing & has_left | (q < 3) & sends_load(q + 1, -1)))
            def _():
                load_copy(q + 1, -1, to, step).start()

            @pl.when(onward & (handing & has_right | (q < 3) & sends_load(q + 1, 1)))
            def _():
                load_copy(q + 1, 1, to, step).start()

        @pl.when(handing)
        def _():
            own_copy().start()

        sends_far = (handing & (l + 1 >= PAIRED)) | ((q == 1) & paired)

        @pl.when(sends_far & far_left & (w == 1))
        def _():
            far_copy(q + 1, -2, to).start()

        @pl.when(sends_far & far_right & (w == TURN - 2))
        def _():
            far_copy(q + 1, 2, to).start()

        @pl.when(at_turn & (lax.rem(q, 2) == 0))
        def _():
            @pl.when(q == 0)
            def _():
                for copy in turn_copies():
                    copy.wait_recv()

            window = jnp.where(turn_left, FAR_LEFT, OWN)
            into = jnp.where(turn_left, LEFT, RIGHT)
            for b in range(NB):
                acc[b] = product(q, window, other, b, REMOTE, [4, 5, 6, 7])

            @pl.when(turn_left)
            def _():
                far_copy(q, 2, l).wait_recv()

            @pl.when(turn_right)
            def _():
                far_copy(q, -2, l).wait_recv()

            for b in range(NB):
                total = acc[b] + product(q, window, other, b, 0, places(b)[:REMOTE])
                re, im = combine(total)
                there = [s_other[q // 2, part, pl.ds(b, 16, stride=4), :] for part in range(2)]
                ext[q + 1, into + b, 0:16] = (there[0] + re).astype(BF16)
                ext[q + 1, into + b, 16:32] = (there[1] + im).astype(BF16)

        @pl.when(lax.rem(q, 2) == 1)
        def _():
            publish(q)
            publish(q - 1)

        return carry

    lax.fori_loop(0, 4, plane, 0)

    load_w.wait()

    @pl.when(jnp.logical_not(first))
    def _():
        layer_copy(1).wait_recv()

    @pl.when(jnp.logical_not(last))
    def _():
        layer_copy(-1).wait_recv()

    for b in range(NB):
        for part in range(2):
            xs[0, part, b] = xlay[0, b, part * 16 : part * 16 + 16].astype(F32)
            xs[5, part, b] = xlay[1, b, part * 16 : part * 16 + 16].astype(F32)

    lane = lax.broadcasted_iota(jnp.int32, (16, 128), 1)

    def residual(q, carry):
        @pl.when(has_left)
        def _():
            x_copy(q, 1).wait_recv()

        @pl.when(has_right)
        def _():
            x_copy(q, -1).wait_recv()

        for b in range(NB):
            s_re = 6.0 - sh_v[q, pl.ds(b, 1), :]
            s_im = sh_v[q, pl.ds(4 + b, 1), :]
            x = [xs[q + 1, part, b] for part in range(2)]
            for part in range(2):
                up = pltpu.roll(x[part], 1, 1)
                before = pltpu.roll(xs[q + 1, part, b - 1], 1, 1) if b > 0 else jnp.zeros_like(up)
                down = pltpu.roll(x[part], 127, 1)
                after = pltpu.roll(xs[q + 1, part, b + 1], 127, 1) if b < 3 else jnp.zeros_like(up)
                beside = jnp.where(lane == 0, before, up) + jnp.where(lane == 127, after, down)
                beside = beside + xs[q, part, b] + xs[q + 2, part, b]
                half = slice(part * 16, part * 16 + 16)
                beside = beside + xh[q, 0, b, half].astype(F32) + xh[q, 1, b, half].astype(F32)
                cross = s_im * x[1] if part == 0 else -(s_im * x[0])
                value = s_re * x[part] + cross - beside
                res_v[q, part, pl.ds(b, 16, stride=4), :] = source(q, part, b) - value
        pltpu.make_async_copy(res_v.at[q], res.at[q], osem.at[1, q]).start()
        return carry

    lax.fori_loop(0, 4, residual, 0)

    for c in range(CUTS):
        @pl.when(first & has_left)
        def _():
            load_copy(0, -1, l, c).wait_send()

        @pl.when(first & has_right)
        def _():
            load_copy(0, 1, l, c).wait_send()

    @pl.when(jnp.logical_not(first))
    def _():
        source_copy().wait_send()
        layer_copy(-1).wait_send()

    @pl.when(jnp.logical_not(last))
    def _():
        own_copy().wait_send()
        layer_copy(1).wait_send()

    @pl.when(at_turn)
    def _():
        for copy in turn_copies():
            copy.wait_send()

    @pl.when(paired & (far_left & (w == 1) | far_right & (w == TURN - 2)))
    def _():
        far_copy(2, 2, l).wait_send()

    @pl.when(jnp.logical_not(last) & (l + 1 >= PAIRED) & (far_left & (w == 1) | far_right & (w == TURN - 2)))
    def _():
        far_copy(4, 2, l).wait_send()

    def drain(q, carry):
        @pl.when(has_left)
        def _():
            x_copy(q, -1).wait_send()

        @pl.when(has_right)
        def _():
            x_copy(q, 1).wait_send()

        handing = (q == 3) & jnp.logical_not(last)
        for c in range(CUTS):
            @pl.when(handing & has_left | (q < 3) & sends_load(q + 1, -1))
            def _():
                load_copy(q + 1, -1, l, c).wait_send()

            @pl.when(handing & has_right | (q < 3) & sends_load(q + 1, 1))
            def _():
                load_copy(q + 1, 1, l, c).wait_send()

        pltpu.make_async_copy(sol_v.at[q], sol.at[q], osem.at[0, q]).wait()
        pltpu.make_async_copy(res_v.at[q], res.at[q], osem.at[1, q]).wait()
        return carry

    lax.fori_loop(0, 4, drain, 0)


def per_device(layers, tiles, source_field, wave_shift, frontal_blocks, block_columns):
    field = jax.ShapeDtypeStruct((4, 2, 64, 128), F32)
    hbm = pl.BlockSpec(memory_space=pltpu.HBM)
    anywhere = pl.BlockSpec(memory_space=pl.ANY)
    dma = pltpu.SemaphoreType.DMA
    sol, res = pl.pallas_call(
        functools.partial(kernel, layers, tiles),
        out_shape=(field, field),
        in_specs=[hbm, hbm, hbm, hbm],
        out_specs=(anywhere, anywhere),
        scratch_shapes=[
            pltpu.VMEM((5, 2, 64, 128), F32),
            pltpu.VMEM((4, 8, 128), F32),
            pltpu.VMEM((4, 8, 2, 128, 128), BF16),
            pltpu.SMEM((4, 8), jnp.int32),
            pltpu.VMEM((4, 1152, 256), BF16),
            pltpu.VMEM((4, 1152, 256), BF16),
            pltpu.VMEM((2, 2, 64, 128), F32),
            pltpu.VMEM((5, 20, 32, 128), BF16),
            pltpu.VMEM((4, 4, 32, 128), BF16),
            pltpu.VMEM((4, 2, 4, 32, 128), BF16),
            pltpu.VMEM((2, 4, 32, 128), BF16),
            pltpu.VMEM((6, 2, 4, 16, 128), F32),
            pltpu.VMEM((4, 32, 256), F32),
            pltpu.VMEM((4, 2, 64, 128), F32),
            pltpu.VMEM((4, 2, 64, 128), F32),
            dma((7,)),
            dma((5, 2, CUTS)),
            dma((4, 2, CUTS)),
            dma((5,)),
            dma((4,)),
            dma((4, 2)),
            dma((4, 2)),
            dma((4,)),
            dma((4,)),
            dma((3,)),
            dma((3,)),
            dma((2, 4)),
        ],
        compiler_params=pltpu.CompilerParams(
            collective_id=0, has_side_effects=True, vmem_limit_bytes=32 * 1024 * 1024
        ),
    )(
        *[
            pltpu.with_memory_space_constraint(operand, pltpu.HBM)
            for operand in (
                source_field.reshape(4, 2, 64, 128),
                wave_shift.reshape(4, 8, 128),
                frontal_blocks[0],
                block_columns[0],
            )
        ]
    )
    return sol.reshape(4, 2, 16, 1, 512), res.reshape(4, 2, 16, 1, 512)


def solution(mesh):
    placed = (
        P("layer", None, None, "tile", None),
        P("layer", None, "tile", None),
        P("layer", "tile", None, None, None, None),
        P("layer", "tile", None),
    )
    return jax.shard_map(
        functools.partial(per_device, mesh.shape["layer"], mesh.shape["tile"]),
        mesh=mesh,
        in_specs=placed,
        out_specs=(P("layer", None, None, "tile", None), P("layer", None, None, "tile", None)),
        check_vma=False,
    )
```

```python
import functools

import jax
import jax.numpy as jnp
from jax import lax
from jax.experimental import pallas as pl
from jax.experimental.pallas import tpu as pltpu
from jax.sharding import PartitionSpec as P

MESH = pl.DeviceIdType.MESH
F32, BF16 = jnp.float32, jnp.bfloat16
NB = 4
TURN = 8
PAIRED = 1
ROUTE = {7: (-2, -3), 4: (3, 6), 2: (-6, -2), 0: (2, 3), 3: (-3, -6), 5: (6, 2)}
ROUTED = 5
SPAN = 288
FAR_LEFT, LEFT, OWN, RIGHT, FAR_RIGHT = 0, 4, 8, 12, 16
CUTS = 2
PIECE = NB // CUTS
REMOTE = 5


def stages(b):
    return [
        [c for c in range(4 - PIECE * (j + 1), 4 - PIECE * j) if c >= b]
        + [8 + c for c in range(PIECE * j, PIECE * (j + 1)) if c <= b]
        for j in range(CUTS)
    ]


def places(b):
    return [c for stage in stages(b) for c in stage] + [4, 5, 6, 7]


def kernel(
    layers, tiles, src, shift, fro, columns, sol, res,
    s_v, sh_v, fro_v, col, dense, other, s_other, ext, xo, xh, xlay, xs, acc, sol_v, res_v,
    lsem, lsend, lrecv, fsend, frecv, xsend, xrecv, csend, crecv, gsend, grecv, rsend, rrecv, osem,
):
    l, t = lax.axis_index("layer"), lax.axis_index("tile")
    first, last = l == 0, l == layers - 1
    has_left, has_right = t > 0, t < tiles - 1
    w = lax.rem(t, TURN)
    turn_left, turn_right = has_left & (w == 0), has_right & (w == TURN - 1)
    far_left = (t > 1) & (w <= 1)
    far_right = (t < tiles - 2) & (w >= TURN - 2)
    far = jnp.where(far_right, 2, -2)
    paired = l >= PAIRED
    onto_next = (w == 7) | (w == 4) | (w == 5)
    on_route = paired & ((onto_next & (t < tiles - TURN)) | (((w == 0) | (w == 2) | (w == 3)) & (t >= TURN)))
    route_from = t + sum(jnp.where(w == place, ROUTE[place][0], 0) for place in ROUTE)
    route_to = t + sum(jnp.where(w == place, ROUTE[place][1], 0) for place in ROUTE)

    barrier = pltpu.get_barrier_semaphore()
    for dl in (0, -1, 1):
        layer_there = (l + dl >= 0) & (l + dl < layers)
        for dt in (-1, 0, 1):
            if dl == 0 and dt == 0:
                continue
            there = layer_there & (t + dt >= 0) & (t + dt < tiles)

            @pl.when(there)
            def _():
                pl.semaphore_signal(barrier, inc=1, device_id=(l + dl, t + dt), device_id_type=MESH)

    for dl in (0, -1, 1):
        layer_there = (l + dl >= 0) & (l + dl < layers)

        @pl.when(layer_there & (far_left | far_right) & (l + max(dl, 0) >= PAIRED))
        def _():
            pl.semaphore_signal(barrier, inc=1, device_id=(l + dl, t + far), device_id_type=MESH)

    @pl.when(on_route)
    def _():
        for there in (route_from, route_to):
            pl.semaphore_signal(barrier, inc=1, device_id=(l, there), device_id_type=MESH)

    load_c = pltpu.make_async_copy(columns, col, lsem.at[0])
    load_s = pltpu.make_async_copy(src, s_v.at[pl.ds(0, 4)], lsem.at[1])
    load_w = pltpu.make_async_copy(shift, sh_v, lsem.at[2])
    load_f = [pltpu.make_async_copy(fro.at[b], fro_v.at[b], lsem.at[3 + b]) for b in range(NB)]
    load_c.start()
    load_f[0].start()
    load_s.start()
    for b in range(1, NB):
        load_f[b].start()
    load_w.start()

    @pl.when(jnp.logical_not(has_left))
    def _():
        ext[:, LEFT : LEFT + 4] = jnp.zeros((5, 4, 32, 128), BF16)
        xh[:, 0] = jnp.zeros((4, 4, 32, 128), BF16)

    @pl.when(jnp.logical_not(has_right))
    def _():
        ext[:, RIGHT : RIGHT + 4] = jnp.zeros((5, 4, 32, 128), BF16)
        xh[:, 1] = jnp.zeros((4, 4, 32, 128), BF16)

    @pl.when(first)
    def _():
        xlay[0] = jnp.zeros((4, 32, 128), BF16)

    @pl.when(last)
    def _():
        xlay[1] = jnp.zeros((4, 32, 128), BF16)
        s_v[4] = jnp.zeros((2, 64, 128), F32)

    def source(q, part, b):
        return s_v[q, part, pl.ds(b, 16, stride=4), :]

    load_c.wait()
    for b in range(NB):
        load_f[b].wait()
        hit = [[col[b, k] == c - b for k in range(8)] for c in places(b)]

        def densify(i, carry, b=b, hit=hit):
            r = pl.multiple_of(i * 16, 16)
            for part in range(2):
                blocks = [fro_v[b, k, part, pl.ds(r, 16), :].astype(F32) for k in range(8)]
                for place in range(9):
                    total = jnp.where(hit[place][0], blocks[0], 0.0)
                    for k in range(1, 8):
                        total = total + jnp.where(hit[place][k], blocks[k], 0.0)
                    dense[b, pl.ds(pl.multiple_of(place * 128 + r, 16), 16), part * 128 : part * 128 + 128] = total.astype(BF16)
            return carry

        lax.fori_loop(0, 8, densify, 0)

    load_s.wait()

    @pl.when(first)
    def _():
        for b in range(NB):
            ext[0, OWN + b, 0:16] = source(0, 0, b).astype(BF16)
            ext[0, OWN + b, 16:32] = source(0, 1, b).astype(BF16)

    rows = jnp.where(first | last, 2, 3)
    cols = jnp.where(has_left & has_right, 3, 2)
    far_rows = sum(
        jnp.where((l + dl >= 0) & (l + dl < layers) & (l + max(dl, 0) >= PAIRED), 1, 0) for dl in (0, -1, 1)
    )
    pl.semaphore_wait(barrier, rows * cols - 1 + jnp.where(far_left | far_right, far_rows, 0) + jnp.where(on_route, 2, 0))

    def load_copy(q, dt, to, j):
        into = LEFT if dt == 1 else RIGHT
        c = 4 - PIECE * (j + 1) if dt == 1 else PIECE * j
        return pltpu.make_async_remote_copy(
            src_ref=ext.at[q, pl.ds(OWN + c, PIECE)],
            dst_ref=ext.at[lax.rem(q, 4), pl.ds(into + c, PIECE)],
            send_sem=lsend.at[q, (1 + dt) // 2, j],
            recv_sem=lrecv.at[lax.rem(q, 4), (1 - dt) // 2, j],
            device_id=(to, t + dt),
            device_id_type=MESH,
        )

    def own_copy():
        return pltpu.make_async_remote_copy(
            src_ref=ext.at[4, pl.ds(OWN, 4)],
            dst_ref=ext.at[0, pl.ds(OWN, 4)],
            send_sem=csend.at[3],
            recv_sem=crecv.at[3],
            device_id=(l + 1, t),
            device_id_type=MESH,
        )

    def far_copy(q, dt, to):
        return pltpu.make_async_remote_copy(
            src_ref=ext.at[q, pl.ds(OWN, 4)],
            dst_ref=ext.at[lax.rem(q, 4), pl.ds(FAR_LEFT if dt == 2 else FAR_RIGHT, 4)],
            send_sem=fsend.at[q],
            recv_sem=frecv.at[lax.rem(q, 4)],
            device_id=(to, t + dt),
            device_id_type=MESH,
        )

    def x_copy(q, dt):
        side = (1 - dt) // 2
        return pltpu.make_async_remote_copy(
            src_ref=xo.at[q],
            dst_ref=xh.at[q, side],
            send_sem=xsend.at[q, side],
            recv_sem=xrecv.at[q, side],
            device_id=(l, t + dt),
            device_id_type=MESH,
        )

    def layer_copy(dl):
        side = (1 - dl) // 2
        return pltpu.make_async_remote_copy(
            src_ref=xo.at[3 if dl == 1 else 0],
            dst_ref=xlay.at[side],
            send_sem=csend.at[side],
            recv_sem=crecv.at[side],
            device_id=(l + dl, t),
            device_id_type=MESH,
        )

    def source_copy():
        return pltpu.make_async_remote_copy(
            src_ref=s_v.at[0],
            dst_ref=s_v.at[4],
            send_sem=csend.at[2],
            recv_sem=crecv.at[2],
            device_id=(l - 1, t),
            device_id_type=MESH,
        )

    across = t + jnp.where(turn_left, -1, 1)

    def turn_copies():
        rest = pl.ds(0, (16 - ROUTED) % 4 * SPAN)
        whole = pl.ds(0, (16 - ROUTED) // 4)
        pieces = [
            (dense.at[(16 - ROUTED) // 4, rest], other.at[(16 - ROUTED) // 4, rest]),
            (dense.at[whole], other.at[whole]),
            (s_v.at[1], s_other.at[0]),
            (s_v.at[3], s_other.at[1]),
        ]
        return [
            pltpu.make_async_remote_copy(
                src_ref=here,
                dst_ref=there,
                send_sem=gsend.at[i],
                recv_sem=grecv.at[i],
                device_id=(l, across),
                device_id_type=MESH,
            )
            for i, (here, there) in enumerate(pieces)
        ]

    at_turn = paired & (turn_left | turn_right)

    def route_copy(k, here):
        i = 15 - k
        piece = (i // 4, pl.ds(i % 4 * SPAN, SPAN))
        return pltpu.make_async_remote_copy(
            src_ref=here.at[piece],
            dst_ref=other.at[piece],
            send_sem=rsend.at[k],
            recv_sem=rrecv.at[k],
            device_id=(l, route_to),
            device_id_type=MESH,
        )

    def sends_load(q, dt):
        there = has_left if dt == -1 else has_right
        turn = turn_left if dt == -1 else turn_right
        return there & jnp.logical_not(paired & turn & (lax.rem(q, 2) == 1))

    for step in range(CUTS):
        @pl.when(first & has_left)
        def _():
            load_copy(0, -1, l, step).start()

        @pl.when(first & has_right)
        def _():
            load_copy(0, 1, l, step).start()

    @pl.when(jnp.logical_not(first))
    def _():
        source_copy().start()

    @pl.when(at_turn)
    def _():
        for copy in turn_copies()[:1:-1]:
            copy.start()
        for k in range(ROUTED):
            route_copy(k, dense).start()
        for copy in turn_copies()[1::-1]:
            copy.start()

    @pl.when(on_route & jnp.logical_not(at_turn))
    def _():
        for k in range(ROUTED):
            route_copy(k, other).wait_recv()
            route_copy(k, other).start()

    def product(q, window, matrix, b, start, blocks):
        operand = jnp.concatenate([ext[q, window + c] for c in blocks], axis=1)
        return jnp.dot(
            operand,
            matrix[b, start * 128 : (start + len(blocks)) * 128],
            preferred_element_type=F32,
        )

    def combine(total):
        re = total[0:16, 0:128] - total[16:32, 128:256]
        im = total[0:16, 128:256] + total[16:32, 0:128]
        return re, im

    def publish(q):
        for b in range(NB):
            for part in range(2):
                xo[q, b, part * 16 : part * 16 + 16] = xs[q + 1, part, b].astype(BF16)

        @pl.when(has_left)
        def _():
            x_copy(q, -1).start()

        @pl.when(has_right)
        def _():
            x_copy(q, 1).start()

        @pl.when((q == 0) & jnp.logical_not(first))
        def _():
            layer_copy(-1).start()

        @pl.when((q == 3) & jnp.logical_not(last))
        def _():
            layer_copy(1).start()

        for b in range(NB):
            for part in range(2):
                sol_v[q, part, pl.ds(b, 16, stride=4), :] = xs[q + 1, part, b]
        pltpu.make_async_copy(sol_v.at[q], sol.at[q], osem.at[0, q]).start()

    def plane(q, carry):
        @pl.when(jnp.logical_not(first) & (q == 0))
        def _():
            own_copy().wait_recv()

        for b in range(NB):
            acc[b] = product(q, LEFT, dense, b, REMOTE, [4, 5, 6, 7])

        @pl.when((q == 3) & jnp.logical_not(last))
        def _():
            source_copy().wait_recv()

        for j in range(CUTS):
            @pl.when(sends_load(q, -1))
            def _():
                load_copy(q, 1, l, j).wait_recv()

            @pl.when(sends_load(q, 1))
            def _():
                load_copy(q, -1, l, j).wait_recv()

            for b in range(NB):
                needs = stages(b)[j]
                if not needs:
                    continue
                start = sum(len(s) for s in stages(b)[:j])
                total = acc[b] + product(q, LEFT, dense, b, start, needs)
                if any(stages(b)[j + 1 :]):
                    acc[b] = total
                    continue
                re, im = combine(total)
                ext[q + 1, OWN + b, 0:16] = (source(q + 1, 0, b) + re).astype(BF16)
                ext[q + 1, OWN + b, 16:32] = (source(q + 1, 1, b) + im).astype(BF16)
                xs[q + 1, 0, b] = re
                xs[q + 1, 1, b] = im

        handing = (q == 3) & jnp.logical_not(last)
        onward = (q < 3) | jnp.logical_not(last)
        to = l + q // 3

        for step in range(CUTS):
            @pl.when(onward & (handing & has_left | (q < 3) & sends_load(q + 1, -1)))
            def _():
                load_copy(q + 1, -1, to, step).start()

            @pl.when(onward & (handing & has_right | (q < 3) & sends_load(q + 1, 1)))
            def _():
                load_copy(q + 1, 1, to, step).start()

        @pl.when(handing)
        def _():
            own_copy().start()

        sends_far = (handing & (l + 1 >= PAIRED)) | ((q == 1) & paired)

        @pl.when(sends_far & far_left & (w == 1))
        def _():
            far_copy(q + 1, -2, to).start()

        @pl.when(sends_far & far_right & (w == TURN - 2))
        def _():
            far_copy(q + 1, 2, to).start()

        @pl.when(at_turn & (lax.rem(q, 2) == 0))
        def _():
            @pl.when(q == 0)
            def _():
                for copy in turn_copies():
                    copy.wait_recv()
                for k in range(ROUTED):
                    route_copy(k, dense).wait_recv()

            window = jnp.where(turn_left, FAR_LEFT, OWN)
            into = jnp.where(turn_left, LEFT, RIGHT)
            for b in range(NB):
                acc[b] = product(q, window, other, b, REMOTE, [4, 5, 6, 7])

            @pl.when(turn_left)
            def _():
                far_copy(q, 2, l).wait_recv()

            @pl.when(turn_right)
            def _():
                far_copy(q, -2, l).wait_recv()

            for b in range(NB):
                total = acc[b] + product(q, window, other, b, 0, places(b)[:REMOTE])
                re, im = combine(total)
                there = [s_other[q // 2, part, pl.ds(b, 16, stride=4), :] for part in range(2)]
                ext[q + 1, into + b, 0:16] = (there[0] + re).astype(BF16)
                ext[q + 1, into + b, 16:32] = (there[1] + im).astype(BF16)

        @pl.when(lax.rem(q, 2) == 1)
        def _():
            publish(q)
            publish(q - 1)

        return carry

    lax.fori_loop(0, 4, plane, 0)

    load_w.wait()

    @pl.when(jnp.logical_not(first))
    def _():
        layer_copy(1).wait_recv()

    @pl.when(jnp.logical_not(last))
    def _():
        layer_copy(-1).wait_recv()

    for b in range(NB):
        for part in range(2):
            xs[0, part, b] = xlay[0, b, part * 16 : part * 16 + 16].astype(F32)
            xs[5, part, b] = xlay[1, b, part * 16 : part * 16 + 16].astype(F32)

    lane = lax.broadcasted_iota(jnp.int32, (16, 128), 1)

    def residual(q, carry):
        @pl.when(has_left)
        def _():
            x_copy(q, 1).wait_recv()

        @pl.when(has_right)
        def _():
            x_copy(q, -1).wait_recv()

        for b in range(NB):
            s_re = 6.0 - sh_v[q, pl.ds(b, 1), :]
            s_im = sh_v[q, pl.ds(4 + b, 1), :]
            x = [xs[q + 1, part, b] for part in range(2)]
            for part in range(2):
                up = pltpu.roll(x[part], 1, 1)
                before = pltpu.roll(xs[q + 1, part, b - 1], 1, 1) if b > 0 else jnp.zeros_like(up)
                down = pltpu.roll(x[part], 127, 1)
                after = pltpu.roll(xs[q + 1, part, b + 1], 127, 1) if b < 3 else jnp.zeros_like(up)
                beside = jnp.where(lane == 0, before, up) + jnp.where(lane == 127, after, down)
                beside = beside + xs[q, part, b] + xs[q + 2, part, b]
                half = slice(part * 16, part * 16 + 16)
                beside = beside + xh[q, 0, b, half].astype(F32) + xh[q, 1, b, half].astype(F32)
                cross = s_im * x[1] if part == 0 else -(s_im * x[0])
                value = s_re * x[part] + cross - beside
                res_v[q, part, pl.ds(b, 16, stride=4), :] = source(q, part, b) - value
        pltpu.make_async_copy(res_v.at[q], res.at[q], osem.at[1, q]).start()
        return carry

    lax.fori_loop(0, 4, residual, 0)

    for c in range(CUTS):
        @pl.when(first & has_left)
        def _():
            load_copy(0, -1, l, c).wait_send()

        @pl.when(first & has_right)
        def _():
            load_copy(0, 1, l, c).wait_send()

    @pl.when(jnp.logical_not(first))
    def _():
        source_copy().wait_send()
        layer_copy(-1).wait_send()

    @pl.when(jnp.logical_not(last))
    def _():
        own_copy().wait_send()
        layer_copy(1).wait_send()

    @pl.when(at_turn)
    def _():
        for copy in turn_copies():
            copy.wait_send()

    @pl.when(on_route)
    def _():
        for k in range(ROUTED):
            route_copy(k, dense).wait_send()

    @pl.when(paired & (far_left & (w == 1) | far_right & (w == TURN - 2)))
    def _():
        far_copy(2, 2, l).wait_send()

    @pl.when(jnp.logical_not(last) & (l + 1 >= PAIRED) & (far_left & (w == 1) | far_right & (w == TURN - 2)))
    def _():
        far_copy(4, 2, l).wait_send()

    def drain(q, carry):
        @pl.when(has_left)
        def _():
            x_copy(q, -1).wait_send()

        @pl.when(has_right)
        def _():
            x_copy(q, 1).wait_send()

        handing = (q == 3) & jnp.logical_not(last)
        for c in range(CUTS):
            @pl.when(handing & has_left | (q < 3) & sends_load(q + 1, -1))
            def _():
                load_copy(q + 1, -1, l, c).wait_send()

            @pl.when(handing & has_right | (q < 3) & sends_load(q + 1, 1))
            def _():
                load_copy(q + 1, 1, l, c).wait_send()

        pltpu.make_async_copy(sol_v.at[q], sol.at[q], osem.at[0, q]).wait()
        pltpu.make_async_copy(res_v.at[q], res.at[q], osem.at[1, q]).wait()
        return carry

    lax.fori_loop(0, 4, drain, 0)


def per_device(layers, tiles, source_field, wave_shift, frontal_blocks, block_columns):
    field = jax.ShapeDtypeStruct((4, 2, 64, 128), F32)
    hbm = pl.BlockSpec(memory_space=pltpu.HBM)
    anywhere = pl.BlockSpec(memory_space=pl.ANY)
    dma = pltpu.SemaphoreType.DMA
    sol, res = pl.pallas_call(
        functools.partial(kernel, layers, tiles),
        out_shape=(field, field),
        in_specs=[hbm, hbm, hbm, hbm],
        out_specs=(anywhere, anywhere),
        scratch_shapes=[
            pltpu.VMEM((5, 2, 64, 128), F32),
            pltpu.VMEM((4, 8, 128), F32),
            pltpu.VMEM((4, 8, 2, 128, 128), BF16),
            pltpu.SMEM((4, 8), jnp.int32),
            pltpu.VMEM((4, 1152, 256), BF16),
            pltpu.VMEM((4, 1152, 256), BF16),
            pltpu.VMEM((2, 2, 64, 128), F32),
            pltpu.VMEM((5, 20, 32, 128), BF16),
            pltpu.VMEM((4, 4, 32, 128), BF16),
            pltpu.VMEM((4, 2, 4, 32, 128), BF16),
            pltpu.VMEM((2, 4, 32, 128), BF16),
            pltpu.VMEM((6, 2, 4, 16, 128), F32),
            pltpu.VMEM((4, 32, 256), F32),
            pltpu.VMEM((4, 2, 64, 128), F32),
            pltpu.VMEM((4, 2, 64, 128), F32),
            dma((7,)),
            dma((5, 2, CUTS)),
            dma((4, 2, CUTS)),
            dma((5,)),
            dma((4,)),
            dma((4, 2)),
            dma((4, 2)),
            dma((4,)),
            dma((4,)),
            dma((4,)),
            dma((4,)),
            dma((ROUTED,)),
            dma((ROUTED,)),
            dma((2, 4)),
        ],
        compiler_params=pltpu.CompilerParams(
            collective_id=0, has_side_effects=True, vmem_limit_bytes=32 * 1024 * 1024
        ),
    )(
        *[
            pltpu.with_memory_space_constraint(operand, pltpu.HBM)
            for operand in (
                source_field.reshape(4, 2, 64, 128),
                wave_shift.reshape(4, 8, 128),
                frontal_blocks[0],
                block_columns[0],
            )
        ]
    )
    return sol.reshape(4, 2, 16, 1, 512), res.reshape(4, 2, 16, 1, 512)


def solution(mesh):
    placed = (
        P("layer", None, None, "tile", None),
        P("layer", None, "tile", None),
        P("layer", "tile", None, None, None, None),
        P("layer", "tile", None),
    )
    return jax.shard_map(
        functools.partial(per_device, mesh.shape["layer"], mesh.shape["tile"]),
        mesh=mesh,
        in_specs=placed,
        out_specs=(P("layer", None, None, "tile", None), P("layer", None, None, "tile", None)),
        check_vma=False,
    )
```

```python
import functools

import jax
import jax.numpy as jnp
from jax import lax
from jax.experimental import pallas as pl
from jax.experimental.pallas import tpu as pltpu
from jax.sharding import PartitionSpec as P

MESH = pl.DeviceIdType.MESH
F32, BF16 = jnp.float32, jnp.bfloat16
NB = 4
TURN = 8
PAIRED = 1
ROUTE = {7: (-2, -3), 4: (3, 6), 2: (-6, -2), 0: (2, 3), 3: (-3, -6), 5: (6, 2)}
ROUTED = 6
SPAN = 288
FAR_LEFT, LEFT, OWN, RIGHT, FAR_RIGHT = 0, 4, 8, 12, 16
CUTS = 2
PIECE = NB // CUTS


def stages(v):
    return [[c for c in range(4 - PIECE * (j + 1), 4 - PIECE * j) if c >= v] for j in range(CUTS)]


def places(v):
    return [c for stage in stages(v) for c in stage] + list(range(8, 9 + v)) + [4, 5, 6, 7]


def kernel(
    layers, tiles, src, shift, fro, columns, sol, res,
    s_v, sh_v, fro_v, col, dense, other, s_other, ext, xo, xh, xlay, xs, acc, other_acc, sol_v, res_v,
    lsem, lsend, lrecv, esend, erecv, fsend, frecv, xsend, xrecv, csend, crecv, gsend, grecv, rsend, rrecv, osem,
):
    l, t = lax.axis_index("layer"), lax.axis_index("tile")
    first, last = l == 0, l == layers - 1
    has_left, has_right = t > 0, t < tiles - 1
    w = lax.rem(t, TURN)
    plain = lax.rem(t, 2) == 0
    where_is = [jnp.where(plain, p, 19 - p) for p in range(16)]
    row_of = [jnp.where(plain, b, 3 - b) for b in range(NB)]
    late = jnp.where(plain, -1, 1)
    has_late = jnp.where(plain, t, tiles - 1 - t) > 0
    turn_left, turn_right = has_left & (w == 0), has_right & (w == TURN - 1)
    far_left = (t > 1) & (w <= 1)
    far_right = (t < tiles - 2) & (w >= TURN - 2)
    far = jnp.where(far_right, 2, -2)
    paired = l >= PAIRED
    onto_next = (w == 7) | (w == 4) | (w == 5)
    on_route = paired & ((onto_next & (t < tiles - TURN)) | (((w == 0) | (w == 2) | (w == 3)) & (t >= TURN)))
    route_from = t + sum(jnp.where(w == place, ROUTE[place][0], 0) for place in ROUTE)
    route_to = t + sum(jnp.where(w == place, ROUTE[place][1], 0) for place in ROUTE)

    barrier = pltpu.get_barrier_semaphore()
    for dl in (0, -1, 1):
        layer_there = (l + dl >= 0) & (l + dl < layers)
        for dt in (-1, 0, 1):
            if dl == 0 and dt == 0:
                continue
            there = layer_there & (t + dt >= 0) & (t + dt < tiles)

            @pl.when(there)
            def _():
                pl.semaphore_signal(barrier, inc=1, device_id=(l + dl, t + dt), device_id_type=MESH)

    for dl in (0, -1, 1):
        layer_there = (l + dl >= 0) & (l + dl < layers)

        @pl.when(layer_there & (far_left | far_right) & (l + max(dl, 0) >= PAIRED))
        def _():
            pl.semaphore_signal(barrier, inc=1, device_id=(l + dl, t + far), device_id_type=MESH)

    @pl.when(on_route)
    def _():
        for there in (route_from, route_to):
            pl.semaphore_signal(barrier, inc=1, device_id=(l, there), device_id_type=MESH)

    load_c = pltpu.make_async_copy(columns, col, lsem.at[0])
    load_s = pltpu.make_async_copy(src, s_v.at[pl.ds(0, 4)], lsem.at[1])
    load_w = pltpu.make_async_copy(shift, sh_v, lsem.at[2])
    load_f = [pltpu.make_async_copy(fro.at[row_of[v]], fro_v.at[v], lsem.at[3 + v]) for v in range(NB)]
    load_c.start()
    load_f[0].start()
    load_s.start()
    for b in range(1, NB):
        load_f[b].start()
    load_w.start()

    @pl.when(jnp.logical_not(has_left))
    def _():
        ext[:, LEFT : LEFT + 4] = jnp.zeros((5, 4, 32, 128), BF16)
        xh[:, 0] = jnp.zeros((4, 4, 32, 128), BF16)

    @pl.when(jnp.logical_not(has_right))
    def _():
        ext[:, RIGHT : RIGHT + 4] = jnp.zeros((5, 4, 32, 128), BF16)
        xh[:, 1] = jnp.zeros((4, 4, 32, 128), BF16)

    @pl.when(first)
    def _():
        xlay[0] = jnp.zeros((4, 32, 128), BF16)

    @pl.when(last)
    def _():
        xlay[1] = jnp.zeros((4, 32, 128), BF16)
        s_v[4] = jnp.zeros((2, 64, 128), F32)

    def source(q, part, b):
        return s_v[q, part, pl.ds(b, 16, stride=4), :]

    load_c.wait()
    for v in range(NB):
        load_f[v].wait()
        hit = [
            [col[row_of[v], k] == jnp.where(plain, c - v, 8 + v - c) for k in range(8)] for c in places(v)
        ]

        def densify(i, carry, v=v, hit=hit):
            r = pl.multiple_of(i * 16, 16)
            for part in range(2):
                blocks = [fro_v[v, k, part, pl.ds(r, 16), :].astype(F32) for k in range(8)]
                for place in range(9):
                    total = jnp.where(hit[place][0], blocks[0], 0.0)
                    for k in range(1, 8):
                        total = total + jnp.where(hit[place][k], blocks[k], 0.0)
                    dense[v, pl.ds(pl.multiple_of(place * 128 + r, 16), 16), part * 128 : part * 128 + 128] = total.astype(BF16)
            return carry

        lax.fori_loop(0, 8, densify, 0)

    load_s.wait()

    @pl.when(first)
    def _():
        for b in range(NB):
            ext[0, OWN + b, 0:16] = source(0, 0, b).astype(BF16)
            ext[0, OWN + b, 16:32] = source(0, 1, b).astype(BF16)

    rows = jnp.where(first | last, 2, 3)
    cols = jnp.where(has_left & has_right, 3, 2)
    far_rows = sum(
        jnp.where((l + dl >= 0) & (l + dl < layers) & (l + max(dl, 0) >= PAIRED), 1, 0) for dl in (0, -1, 1)
    )
    pl.semaphore_wait(barrier, rows * cols - 1 + jnp.where(far_left | far_right, far_rows, 0) + jnp.where(on_route, 2, 0))

    def late_copy(q, to, j):
        c = jnp.where(plain, PIECE * j, 4 - PIECE * (j + 1))
        return pltpu.make_async_remote_copy(
            src_ref=ext.at[q, pl.ds(OWN + c, PIECE)],
            dst_ref=ext.at[lax.rem(q, 4), pl.ds(jnp.where(plain, RIGHT, LEFT) + c, PIECE)],
            send_sem=lsend.at[q, j],
            recv_sem=lrecv.at[lax.rem(q, 4), j],
            device_id=(to, t + late),
            device_id_type=MESH,
        )

    def early_copy(q, to):
        return pltpu.make_async_remote_copy(
            src_ref=ext.at[q, pl.ds(OWN, 4)],
            dst_ref=ext.at[lax.rem(q, 4), pl.ds(jnp.where(plain, LEFT, RIGHT), 4)],
            send_sem=esend.at[q],
            recv_sem=erecv.at[lax.rem(q, 4)],
            device_id=(to, t - late),
            device_id_type=MESH,
        )

    def own_copy():
        return pltpu.make_async_remote_copy(
            src_ref=ext.at[4, pl.ds(OWN, 4)],
            dst_ref=ext.at[0, pl.ds(OWN, 4)],
            send_sem=csend.at[3],
            recv_sem=crecv.at[3],
            device_id=(l + 1, t),
            device_id_type=MESH,
        )

    def far_copy(q, dt, to):
        return pltpu.make_async_remote_copy(
            src_ref=ext.at[q, pl.ds(OWN, 4)],
            dst_ref=ext.at[lax.rem(q, 4), pl.ds(FAR_LEFT if dt == 2 else FAR_RIGHT, 4)],
            send_sem=fsend.at[q],
            recv_sem=frecv.at[lax.rem(q, 4)],
            device_id=(to, t + dt),
            device_id_type=MESH,
        )

    def x_copy(q, dt):
        side = (1 - dt) // 2
        return pltpu.make_async_remote_copy(
            src_ref=xo.at[q],
            dst_ref=xh.at[q, side],
            send_sem=xsend.at[q, side],
            recv_sem=xrecv.at[q, side],
            device_id=(l, t + dt),
            device_id_type=MESH,
        )

    def layer_copy(dl):
        side = (1 - dl) // 2
        return pltpu.make_async_remote_copy(
            src_ref=xo.at[3 if dl == 1 else 0],
            dst_ref=xlay.at[side],
            send_sem=csend.at[side],
            recv_sem=crecv.at[side],
            device_id=(l + dl, t),
            device_id_type=MESH,
        )

    def source_copy():
        return pltpu.make_async_remote_copy(
            src_ref=s_v.at[0],
            dst_ref=s_v.at[4],
            send_sem=csend.at[2],
            recv_sem=crecv.at[2],
            device_id=(l - 1, t),
            device_id_type=MESH,
        )

    across = t + jnp.where(turn_left, -1, 1)

    def turn_copies():
        rest = pl.ds(0, (16 - ROUTED) % 4 * SPAN)
        whole = pl.ds(0, (16 - ROUTED) // 4)
        pieces = [
            (dense.at[(16 - ROUTED) // 4, rest], other.at[(16 - ROUTED) // 4, rest]),
            (dense.at[whole], other.at[whole]),
            (s_v.at[1], s_other.at[0]),
            (s_v.at[3], s_other.at[1]),
        ]
        return [
            pltpu.make_async_remote_copy(
                src_ref=here,
                dst_ref=there,
                send_sem=gsend.at[i],
                recv_sem=grecv.at[i],
                device_id=(l, across),
                device_id_type=MESH,
            )
            for i, (here, there) in enumerate(pieces)
        ]

    at_turn = paired & (turn_left | turn_right)

    def route_copy(k, here):
        i = 15 - k
        piece = (i // 4, pl.ds(i % 4 * SPAN, SPAN))
        return pltpu.make_async_remote_copy(
            src_ref=here.at[piece],
            dst_ref=other.at[piece],
            send_sem=rsend.at[k],
            recv_sem=rrecv.at[k],
            device_id=(l, route_to),
            device_id_type=MESH,
        )

    def late_moves(q):
        return has_late & jnp.logical_not(at_turn & (lax.rem(q, 2) == 1))

    @pl.when(first & has_late)
    def _():
        for j in range(CUTS):
            late_copy(0, l, j).start()

    @pl.when(first)
    def _():
        early_copy(0, l).start()

    @pl.when(jnp.logical_not(first))
    def _():
        source_copy().start()

    @pl.when(at_turn)
    def _():
        for copy in turn_copies()[:1:-1]:
            copy.start()
        for k in range(ROUTED):
            route_copy(k, dense).start()
        for copy in turn_copies()[1::-1]:
            copy.start()

    @pl.when(on_route & jnp.logical_not(at_turn))
    def _():
        for k in range(ROUTED):
            route_copy(k, other).wait_recv()
            route_copy(k, other).start()

    def product(q, blocks, matrix, v, start):
        operand = jnp.concatenate([ext[q, where_is[p]] for p in blocks], axis=1)
        return jnp.dot(
            operand,
            matrix[v, start * 128 : (start + len(blocks)) * 128],
            preferred_element_type=F32,
        )

    def combine(total):
        re = total[0:16, 0:128] - total[16:32, 128:256]
        im = total[0:16, 128:256] + total[16:32, 0:128]
        return re, im

    def publish(q):
        for b in range(NB):
            for part in range(2):
                xo[q, b, part * 16 : part * 16 + 16] = xs[q + 1, part, b].astype(BF16)

        @pl.when(has_left)
        def _():
            x_copy(q, -1).start()

        @pl.when(has_right)
        def _():
            x_copy(q, 1).start()

        @pl.when((q == 0) & jnp.logical_not(first))
        def _():
            layer_copy(-1).start()

        @pl.when((q == 3) & jnp.logical_not(last))
        def _():
            layer_copy(1).start()

        for b in range(NB):
            for part in range(2):
                sol_v[q, part, pl.ds(b, 16, stride=4), :] = xs[q + 1, part, b]
        pltpu.make_async_copy(sol_v.at[q], sol.at[q], osem.at[0, q]).start()

    def plane(q, carry):
        @pl.when(jnp.logical_not(first) & (q == 0))
        def _():
            own_copy().wait_recv()

        early_copy(q, l).wait_recv()
        for v in range(NB):
            acc[v] = product(q, [4 + c for c in places(v)[4 - v :]], dense, v, 4 - v)

        doubles = at_turn & (lax.rem(q, 2) == 0)

        @pl.when(doubles)
        def _():
            @pl.when(q == 0)
            def _():
                for copy in turn_copies():
                    copy.wait_recv()
                for k in range(ROUTED):
                    route_copy(k, dense).wait_recv()

            for v in range(NB):
                other_acc[v] = product(q, [11 - c for c in places(v)[: 4 - v]], other, v, 0)

        @pl.when((q == 3) & jnp.logical_not(last))
        def _():
            source_copy().wait_recv()

        for j in range(CUTS):
            @pl.when(late_moves(q))
            def _():
                late_copy(q, l, j).wait_recv()

            for v in range(NB):
                needs = stages(v)[j]
                if needs:
                    start = sum(len(s) for s in stages(v)[:j])
                    acc[v] += product(q, [4 + c for c in needs], dense, v, start)

        for b in range(NB):
            re, im = combine(acc[row_of[b]])
            ext[q + 1, OWN + b, 0:16] = (source(q + 1, 0, b) + re).astype(BF16)
            ext[q + 1, OWN + b, 16:32] = (source(q + 1, 1, b) + im).astype(BF16)
            xs[q + 1, 0, b] = re
            xs[q + 1, 1, b] = im

        handing = (q == 3) & jnp.logical_not(last)
        onward = (q < 3) | jnp.logical_not(last)
        to = l + q // 3

        @pl.when((handing & has_late) | ((q < 3) & late_moves(q + 1)))
        def _():
            for j in range(CUTS):
                late_copy(q + 1, to, j).start()

        @pl.when(onward)
        def _():
            early_copy(q + 1, to).start()

        @pl.when(handing)
        def _():
            own_copy().start()

        sends_far = (handing & (l + 1 >= PAIRED)) | ((q == 1) & paired)

        @pl.when(sends_far & far_left & (w == 1))
        def _():
            far_copy(q + 1, -2, to).start()

        @pl.when(sends_far & far_right & (w == TURN - 2))
        def _():
            far_copy(q + 1, 2, to).start()

        @pl.when(doubles)
        def _():
            far_copy(q, 2, l).wait_recv()

            for v in range(NB):
                other_acc[v] += product(q, [11 - c for c in places(v)[4 - v :]], other, v, 4 - v)

            into = jnp.where(turn_left, LEFT, RIGHT)
            for b in range(NB):
                re, im = combine(other_acc[3 - row_of[b]])
                there = [s_other[q // 2, part, pl.ds(b, 16, stride=4), :] for part in range(2)]
                ext[q + 1, into + b, 0:16] = (there[0] + re).astype(BF16)
                ext[q + 1, into + b, 16:32] = (there[1] + im).astype(BF16)

        @pl.when(lax.rem(q, 2) == 1)
        def _():
            publish(q)
            publish(q - 1)

        return carry

    lax.fori_loop(0, 4, plane, 0)

    load_w.wait()

    @pl.when(jnp.logical_not(first))
    def _():
        layer_copy(1).wait_recv()

    @pl.when(jnp.logical_not(last))
    def _():
        layer_copy(-1).wait_recv()

    for b in range(NB):
        for part in range(2):
            xs[0, part, b] = xlay[0, b, part * 16 : part * 16 + 16].astype(F32)
            xs[5, part, b] = xlay[1, b, part * 16 : part * 16 + 16].astype(F32)

    lane = lax.broadcasted_iota(jnp.int32, (16, 128), 1)

    def residual(q, carry):
        @pl.when(has_left)
        def _():
            x_copy(q, 1).wait_recv()

        @pl.when(has_right)
        def _():
            x_copy(q, -1).wait_recv()

        for b in range(NB):
            s_re = 6.0 - sh_v[q, pl.ds(b, 1), :]
            s_im = sh_v[q, pl.ds(4 + b, 1), :]
            x = [xs[q + 1, part, b] for part in range(2)]
            for part in range(2):
                up = pltpu.roll(x[part], 1, 1)
                before = pltpu.roll(xs[q + 1, part, b - 1], 1, 1) if b > 0 else jnp.zeros_like(up)
                down = pltpu.roll(x[part], 127, 1)
                after = pltpu.roll(xs[q + 1, part, b + 1], 127, 1) if b < 3 else jnp.zeros_like(up)
                beside = jnp.where(lane == 0, before, up) + jnp.where(lane == 127, after, down)
                beside = beside + xs[q, part, b] + xs[q + 2, part, b]
                half = slice(part * 16, part * 16 + 16)
                beside = beside + xh[q, 0, b, half].astype(F32) + xh[q, 1, b, half].astype(F32)
                cross = s_im * x[1] if part == 0 else -(s_im * x[0])
                value = s_re * x[part] + cross - beside
                res_v[q, part, pl.ds(b, 16, stride=4), :] = source(q, part, b) - value
        pltpu.make_async_copy(res_v.at[q], res.at[q], osem.at[1, q]).start()
        return carry

    lax.fori_loop(0, 4, residual, 0)

    @pl.when(first & has_late)
    def _():
        for j in range(CUTS):
            late_copy(0, l, j).wait_send()

    @pl.when(first)
    def _():
        early_copy(0, l).wait_send()

    @pl.when(jnp.logical_not(first))
    def _():
        source_copy().wait_send()
        layer_copy(-1).wait_send()

    @pl.when(jnp.logical_not(last))
    def _():
        own_copy().wait_send()
        layer_copy(1).wait_send()

    @pl.when(at_turn)
    def _():
        for copy in turn_copies():
            copy.wait_send()

    @pl.when(on_route)
    def _():
        for k in range(ROUTED):
            route_copy(k, dense).wait_send()

    @pl.when(paired & (far_left & (w == 1) | far_right & (w == TURN - 2)))
    def _():
        far_copy(2, 2, l).wait_send()

    @pl.when(jnp.logical_not(last) & (l + 1 >= PAIRED) & (far_left & (w == 1) | far_right & (w == TURN - 2)))
    def _():
        far_copy(4, 2, l).wait_send()

    def drain(q, carry):
        @pl.when(has_left)
        def _():
            x_copy(q, -1).wait_send()

        @pl.when(has_right)
        def _():
            x_copy(q, 1).wait_send()

        handing = (q == 3) & jnp.logical_not(last)

        @pl.when((handing & has_late) | ((q < 3) & late_moves(q + 1)))
        def _():
            for j in range(CUTS):
                late_copy(q + 1, l, j).wait_send()

        @pl.when((q < 3) | handing)
        def _():
            early_copy(q + 1, l).wait_send()

        pltpu.make_async_copy(sol_v.at[q], sol.at[q], osem.at[0, q]).wait()
        pltpu.make_async_copy(res_v.at[q], res.at[q], osem.at[1, q]).wait()
        return carry

    lax.fori_loop(0, 4, drain, 0)


def per_device(layers, tiles, source_field, wave_shift, frontal_blocks, block_columns):
    field = jax.ShapeDtypeStruct((4, 2, 64, 128), F32)
    hbm = pl.BlockSpec(memory_space=pltpu.HBM)
    anywhere = pl.BlockSpec(memory_space=pl.ANY)
    dma = pltpu.SemaphoreType.DMA
    sol, res = pl.pallas_call(
        functools.partial(kernel, layers, tiles),
        out_shape=(field, field),
        in_specs=[hbm, hbm, hbm, hbm],
        out_specs=(anywhere, anywhere),
        scratch_shapes=[
            pltpu.VMEM((5, 2, 64, 128), F32),
            pltpu.VMEM((4, 8, 128), F32),
            pltpu.VMEM((4, 8, 2, 128, 128), BF16),
            pltpu.SMEM((4, 8), jnp.int32),
            pltpu.VMEM((4, 1152, 256), BF16),
            pltpu.VMEM((4, 1152, 256), BF16),
            pltpu.VMEM((2, 2, 64, 128), F32),
            pltpu.VMEM((5, 20, 32, 128), BF16),
            pltpu.VMEM((4, 4, 32, 128), BF16),
            pltpu.VMEM((4, 2, 4, 32, 128), BF16),
            pltpu.VMEM((2, 4, 32, 128), BF16),
            pltpu.VMEM((6, 2, 4, 16, 128), F32),
            pltpu.VMEM((4, 32, 256), F32),
            pltpu.VMEM((4, 32, 256), F32),
            pltpu.VMEM((4, 2, 64, 128), F32),
            pltpu.VMEM((4, 2, 64, 128), F32),
            dma((7,)),
            dma((5, CUTS)),
            dma((4, CUTS)),
            dma((5,)),
            dma((4,)),
            dma((5,)),
            dma((4,)),
            dma((4, 2)),
            dma((4, 2)),
            dma((4,)),
            dma((4,)),
            dma((4,)),
            dma((4,)),
            dma((ROUTED,)),
            dma((ROUTED,)),
            dma((2, 4)),
        ],
        compiler_params=pltpu.CompilerParams(
            collective_id=0, has_side_effects=True, vmem_limit_bytes=32 * 1024 * 1024
        ),
    )(
        *[
            pltpu.with_memory_space_constraint(operand, pltpu.HBM)
            for operand in (
                source_field.reshape(4, 2, 64, 128),
                wave_shift.reshape(4, 8, 128),
                frontal_blocks[0],
                block_columns[0],
            )
        ]
    )
    return sol.reshape(4, 2, 16, 1, 512), res.reshape(4, 2, 16, 1, 512)


def solution(mesh):
    placed = (
        P("layer", None, None, "tile", None),
        P("layer", None, "tile", None),
        P("layer", "tile", None, None, None, None),
        P("layer", "tile", None),
    )
    return jax.shard_map(
        functools.partial(per_device, mesh.shape["layer"], mesh.shape["tile"]),
        mesh=mesh,
        in_specs=placed,
        out_specs=(P("layer", None, None, "tile", None), P("layer", None, None, "tile", None)),
        check_vma=False,
    )
```

```python
import functools

import jax
import jax.numpy as jnp
from jax import lax
from jax.experimental import pallas as pl
from jax.experimental.pallas import tpu as pltpu
from jax.sharding import PartitionSpec as P

MESH = pl.DeviceIdType.MESH
F32, BF16 = jnp.float32, jnp.bfloat16
NB = 4
TURN = 8
PAIRED = 1
ROUTE = {7: (-2, -3), 4: (3, 6), 2: (-6, -2), 0: (2, 3), 3: (-3, -6), 5: (6, 2)}
ROUTED = 6
SPAN = 288
FAR_LEFT, LEFT, OWN, RIGHT, FAR_RIGHT = 0, 4, 8, 12, 16
CUTS = 2
PIECE = NB // CUTS
REMOTE = 5


def stages(v):
    return [[c for c in range(4 - PIECE * (j + 1), 4 - PIECE * j) if c >= v] for j in range(CUTS)]


def places(v):
    return [c for stage in stages(v) for c in stage] + list(range(8, 9 + v)) + [4, 5, 6, 7]


def kernel(
    layers, tiles, src, shift, fro, columns, sol, res,
    s_v, sh_v, fro_v, col, dense, other, s_other, ext, xo, xh, xlay, xs, acc, other_acc,
    lsem, lsend, lrecv, esend, erecv, fsend, frecv, xsend, xrecv, csend, crecv, gsend, grecv, rsend, rrecv,
):
    l, t = lax.axis_index("layer"), lax.axis_index("tile")
    first, last = l == 0, l == layers - 1
    has_left, has_right = t > 0, t < tiles - 1
    w = lax.rem(t, TURN)
    plain = lax.rem(t, 2) == 0
    where_is = [jnp.where(plain, p, 19 - p) for p in range(16)]
    row_of = [jnp.where(plain, b, 3 - b) for b in range(NB)]
    late = jnp.where(plain, -1, 1)
    has_late = jnp.where(plain, t, tiles - 1 - t) > 0
    turn_left, turn_right = has_left & (w == 0), has_right & (w == TURN - 1)
    far_left = (t > 1) & (w <= 1)
    far_right = (t < tiles - 2) & (w >= TURN - 2)
    far = jnp.where(far_right, 2, -2)
    paired = l >= PAIRED
    onto_next = (w == 7) | (w == 4) | (w == 5)
    on_route = paired & ((onto_next & (t < tiles - TURN)) | (((w == 0) | (w == 2) | (w == 3)) & (t >= TURN)))
    route_from = t + sum(jnp.where(w == place, ROUTE[place][0], 0) for place in ROUTE)
    route_to = t + sum(jnp.where(w == place, ROUTE[place][1], 0) for place in ROUTE)

    barrier = pltpu.get_barrier_semaphore()
    for there, dl, dt in (
        (has_left, 0, -1),
        (has_right, 0, 1),
        (paired & (far_left | far_right), 0, far),
        (jnp.logical_not(first), -1, 0),
        (jnp.logical_not(last), 1, 0),
    ):
        @pl.when(there)
        def _():
            pl.semaphore_signal(barrier, inc=1, device_id=(l + dl, t + dt), device_id_type=MESH)

    @pl.when(on_route)
    def _():
        for there in (route_from, route_to):
            pl.semaphore_signal(barrier, inc=1, device_id=(l, there), device_id_type=MESH)

    load_c = pltpu.make_async_copy(columns, col, lsem.at[0])
    load_s = pltpu.make_async_copy(src, s_v.at[pl.ds(0, 4)], lsem.at[1])
    load_w = pltpu.make_async_copy(shift, sh_v, lsem.at[2])
    load_f = [pltpu.make_async_copy(fro.at[row_of[v]], fro_v.at[v], lsem.at[3 + v]) for v in range(NB)]
    load_c.start()
    load_f[0].start()
    load_s.start()
    for b in range(1, NB):
        load_f[b].start()
    load_w.start()

    @pl.when(jnp.logical_not(has_left))
    def _():
        ext[:, LEFT : LEFT + 4] = jnp.zeros((5, 4, 32, 128), BF16)
        xh[:, 0] = jnp.zeros((4, 4, 32, 128), BF16)

    @pl.when(jnp.logical_not(has_right))
    def _():
        ext[:, RIGHT : RIGHT + 4] = jnp.zeros((5, 4, 32, 128), BF16)
        xh[:, 1] = jnp.zeros((4, 4, 32, 128), BF16)

    @pl.when(first)
    def _():
        xlay[0] = jnp.zeros((4, 32, 128), BF16)

    @pl.when(last)
    def _():
        xlay[1] = jnp.zeros((4, 32, 128), BF16)
        s_v[4] = jnp.zeros((2, 64, 128), F32)

    def source(q, part, b):
        return s_v[q, part, pl.ds(b, 16, stride=4), :]

    load_c.wait()
    for v in range(NB):
        load_f[v].wait()
        hit = [
            [col[row_of[v], k] == jnp.where(plain, c - v, 8 + v - c) for k in range(8)] for c in places(v)
        ]

        def densify(i, carry, v=v, hit=hit):
            r = pl.multiple_of(i * 16, 16)
            for part in range(2):
                blocks = [fro_v[v, k, part, pl.ds(r, 16), :].astype(F32) for k in range(8)]
                for place in range(9):
                    total = jnp.where(hit[place][0], blocks[0], 0.0)
                    for k in range(1, 8):
                        total = total + jnp.where(hit[place][k], blocks[k], 0.0)
                    dense[v, pl.ds(pl.multiple_of(place * 128 + r, 16), 16), part * 128 : part * 128 + 128] = total.astype(BF16)
            return carry

        lax.fori_loop(0, 8, densify, 0)

    load_s.wait()

    @pl.when(first)
    def _():
        for b in range(NB):
            ext[0, OWN + b, 0:16] = source(0, 0, b).astype(BF16)
            ext[0, OWN + b, 16:32] = source(0, 1, b).astype(BF16)

    one = lambda there: jnp.where(there, 1, 0)
    pl.semaphore_wait(
        barrier,
        one(has_left) + one(has_right) + one(paired & (far_left | far_right))
        + one(jnp.logical_not(first)) + one(jnp.logical_not(last)) + 2 * one(on_route),
    )

    def late_copy(q, to, j):
        c = jnp.where(plain, PIECE * j, 4 - PIECE * (j + 1))
        return pltpu.make_async_remote_copy(
            src_ref=ext.at[q, pl.ds(OWN + c, PIECE)],
            dst_ref=ext.at[lax.rem(q, 4), pl.ds(jnp.where(plain, RIGHT, LEFT) + c, PIECE)],
            send_sem=lsend.at[q, j],
            recv_sem=lrecv.at[lax.rem(q, 4), j],
            device_id=(to, t + late),
            device_id_type=MESH,
        )

    def early_copy(q, to):
        return pltpu.make_async_remote_copy(
            src_ref=ext.at[q, pl.ds(OWN, 4)],
            dst_ref=ext.at[lax.rem(q, 4), pl.ds(jnp.where(plain, LEFT, RIGHT), 4)],
            send_sem=esend.at[q],
            recv_sem=erecv.at[lax.rem(q, 4)],
            device_id=(to, t - late),
            device_id_type=MESH,
        )

    def own_copy():
        return pltpu.make_async_remote_copy(
            src_ref=ext.at[4, pl.ds(OWN, 4)],
            dst_ref=ext.at[0, pl.ds(OWN, 4)],
            send_sem=csend.at[3],
            recv_sem=crecv.at[3],
            device_id=(l + 1, t),
            device_id_type=MESH,
        )

    def far_copy(q, dt, to):
        return pltpu.make_async_remote_copy(
            src_ref=ext.at[q, pl.ds(OWN, 4)],
            dst_ref=ext.at[lax.rem(q, 4), pl.ds(FAR_LEFT if dt == 2 else FAR_RIGHT, 4)],
            send_sem=fsend.at[q],
            recv_sem=frecv.at[lax.rem(q, 4)],
            device_id=(to, t + dt),
            device_id_type=MESH,
        )

    def x_copy(q, dt):
        side = (1 - dt) // 2
        return pltpu.make_async_remote_copy(
            src_ref=xo.at[q],
            dst_ref=xh.at[q, side],
            send_sem=xsend.at[q, side],
            recv_sem=xrecv.at[q, side],
            device_id=(l, t + dt),
            device_id_type=MESH,
        )

    def layer_copy(dl):
        side = (1 - dl) // 2
        return pltpu.make_async_remote_copy(
            src_ref=xo.at[3 if dl == 1 else 0],
            dst_ref=xlay.at[side],
            send_sem=csend.at[side],
            recv_sem=crecv.at[side],
            device_id=(l + dl, t),
            device_id_type=MESH,
        )

    def source_copy():
        return pltpu.make_async_remote_copy(
            src_ref=s_v.at[0],
            dst_ref=s_v.at[4],
            send_sem=csend.at[2],
            recv_sem=crecv.at[2],
            device_id=(l - 1, t),
            device_id_type=MESH,
        )

    across = t + jnp.where(turn_left, -1, 1)

    def turn_copies():
        rest = pl.ds(0, (16 - ROUTED) % 4 * SPAN)
        whole = pl.ds(0, (16 - ROUTED) // 4)
        pieces = [
            (dense.at[(16 - ROUTED) // 4, rest], other.at[(16 - ROUTED) // 4, rest]),
            (dense.at[whole], other.at[whole]),
            (s_v.at[1], s_other.at[0]),
            (s_v.at[3], s_other.at[1]),
        ]
        return [
            pltpu.make_async_remote_copy(
                src_ref=here,
                dst_ref=there,
                send_sem=gsend.at[i],
                recv_sem=grecv.at[i],
                device_id=(l, across),
                device_id_type=MESH,
            )
            for i, (here, there) in enumerate(pieces)
        ]

    at_turn = paired & (turn_left | turn_right)

    def route_copy(k, here):
        i = 15 - k
        piece = (i // 4, pl.ds(i % 4 * SPAN, SPAN))
        return pltpu.make_async_remote_copy(
            src_ref=here.at[piece],
            dst_ref=other.at[piece],
            send_sem=rsend.at[k],
            recv_sem=rrecv.at[k],
            device_id=(l, route_to),
            device_id_type=MESH,
        )

    def late_moves(q):
        return has_late & jnp.logical_not(at_turn & (lax.rem(q, 2) == 1))

    @pl.when(first & has_late)
    def _():
        for j in range(CUTS):
            late_copy(0, l, j).start()

    @pl.when(first)
    def _():
        early_copy(0, l).start()

    @pl.when(jnp.logical_not(first))
    def _():
        source_copy().start()

    @pl.when(at_turn)
    def _():
        for copy in turn_copies()[:1:-1]:
            copy.start()
        for k in range(ROUTED):
            route_copy(k, dense).start()
        for copy in turn_copies()[1::-1]:
            copy.start()

    @pl.when(on_route & jnp.logical_not(at_turn))
    def _():
        for k in range(ROUTED):
            route_copy(k, other).wait_recv()
            route_copy(k, other).start()

    def product(q, blocks, matrix, v, start):
        operand = jnp.concatenate([ext[q, where_is[p]] for p in blocks], axis=1)
        return jnp.dot(
            operand,
            matrix[v, start * 128 : (start + len(blocks)) * 128],
            preferred_element_type=F32,
        )

    def combine(total):
        re = total[0:16, 0:128] - total[16:32, 128:256]
        im = total[0:16, 128:256] + total[16:32, 0:128]
        return re, im

    def publish(q):
        for b in range(NB):
            for part in range(2):
                xo[q, b, part * 16 : part * 16 + 16] = xs[q + 1, part, b].astype(BF16)

        @pl.when(has_left)
        def _():
            x_copy(q, -1).start()

        @pl.when(has_right)
        def _():
            x_copy(q, 1).start()

        @pl.when((q == 0) & jnp.logical_not(first))
        def _():
            layer_copy(-1).start()

        @pl.when((q == 3) & jnp.logical_not(last))
        def _():
            layer_copy(1).start()

        for b in range(NB):
            for part in range(2):
                sol[q, part, pl.ds(b, 16, stride=4), :] = xs[q + 1, part, b]

    def plane(q, carry):
        @pl.when(jnp.logical_not(first) & (q == 0))
        def _():
            own_copy().wait_recv()

        behind = at_turn & (lax.rem(q, 2) == 1)

        def begin(q):
            early_copy(q, l).wait_recv()
            for v in range(NB):
                acc[v] = product(q, [4 + c for c in places(v)[4 - v :]], dense, v, 4 - v)

        @pl.when(jnp.logical_not(behind))
        def _():
            begin(q)

        doubles = at_turn & (lax.rem(q, 2) == 0)

        @pl.when(doubles)
        def _():
            @pl.when(q == 0)
            def _():
                for copy in turn_copies():
                    copy.wait_recv()
                for k in range(ROUTED):
                    route_copy(k, dense).wait_recv()

            for v in range(NB):
                other_acc[v] = product(q, [11 - c for c in places(v)[: 4 - v]], other, v, 0)

        @pl.when((q == 3) & jnp.logical_not(last))
        def _():
            source_copy().wait_recv()

        def finish(v):
            b = row_of[v]
            re, im = combine(acc[v])
            ext[q + 1, OWN + b, 0:16] = (s_v[q + 1, 0, pl.ds(b, 16, stride=4), :] + re).astype(BF16)
            ext[q + 1, OWN + b, 16:32] = (s_v[q + 1, 1, pl.ds(b, 16, stride=4), :] + im).astype(BF16)
            xs[q + 1, 0, b] = re
            xs[q + 1, 1, b] = im

        @pl.when(behind)
        def _():
            for v in range(NB):
                acc[v] += product(q, [4 + c for c in places(v)[: 4 - v]], dense, v, 0)
            for v in range(PIECE, NB):
                finish(v)

        @pl.when(jnp.logical_not(behind))
        def _():
            for j in range(CUTS):
                @pl.when(has_late)
                def _():
                    late_copy(q, l, j).wait_recv()

                for v in range(NB):
                    needs = stages(v)[j]
                    if needs:
                        start = sum(len(s) for s in stages(v)[:j])
                        acc[v] += product(q, [4 + c for c in needs], dense, v, start)
                if j == 0:
                    for v in range(PIECE, NB):
                        finish(v)

        for v in range(PIECE):
            finish(v)

        handing = (q == 3) & jnp.logical_not(last)
        onward = (q < 3) | jnp.logical_not(last)
        to = l + q // 3

        @pl.when((handing & has_late) | ((q < 3) & late_moves(q + 1)))
        def _():
            for j in range(CUTS):
                late_copy(q + 1, to, j).start()

        @pl.when(onward)
        def _():
            early_copy(q + 1, to).start()

        @pl.when(handing)
        def _():
            own_copy().start()

        sends_far = (handing & (l + 1 >= PAIRED)) | ((q == 1) & paired)

        @pl.when(sends_far & far_left & (w == 1))
        def _():
            far_copy(q + 1, -2, to).start()

        @pl.when(sends_far & far_right & (w == TURN - 2))
        def _():
            far_copy(q + 1, 2, to).start()

        @pl.when(doubles)
        def _():
            begin(q + 1)
            for v in range(NB):
                other_acc[v] += product(q, [11 - c for c in places(v)[REMOTE:]], other, v, REMOTE)
            far_copy(q, 2, l).wait_recv()
            for v in range(NB):
                other_acc[v] += product(q, [11 - c for c in places(v)[4 - v : REMOTE]], other, v, 4 - v)

            into = jnp.where(turn_left, LEFT, RIGHT)
            for b in range(NB):
                re, im = combine(other_acc[3 - row_of[b]])
                there = [s_other[q // 2, part, pl.ds(b, 16, stride=4), :] for part in range(2)]
                ext[q + 1, into + b, 0:16] = (there[0] + re).astype(BF16)
                ext[q + 1, into + b, 16:32] = (there[1] + im).astype(BF16)

        @pl.when(lax.rem(q, 2) == 1)
        def _():
            publish(q)
            publish(q - 1)

        return carry

    lax.fori_loop(0, 4, plane, 0)

    load_w.wait()

    @pl.when(jnp.logical_not(first))
    def _():
        layer_copy(1).wait_recv()

    @pl.when(jnp.logical_not(last))
    def _():
        layer_copy(-1).wait_recv()

    for b in range(NB):
        for part in range(2):
            xs[0, part, b] = xlay[0, b, part * 16 : part * 16 + 16].astype(F32)
            xs[5, part, b] = xlay[1, b, part * 16 : part * 16 + 16].astype(F32)

    lane = lax.broadcasted_iota(jnp.int32, (16, 128), 1)

    def residual(q, carry):
        @pl.when(has_left)
        def _():
            x_copy(q, 1).wait_recv()

        @pl.when(has_right)
        def _():
            x_copy(q, -1).wait_recv()

        for b in range(NB):
            s_re = 6.0 - sh_v[q, pl.ds(b, 1), :]
            s_im = sh_v[q, pl.ds(4 + b, 1), :]
            x = [xs[q + 1, part, b] for part in range(2)]
            for part in range(2):
                up = pltpu.roll(x[part], 1, 1)
                before = pltpu.roll(xs[q + 1, part, b - 1], 1, 1) if b > 0 else jnp.zeros_like(up)
                down = pltpu.roll(x[part], 127, 1)
                after = pltpu.roll(xs[q + 1, part, b + 1], 127, 1) if b < 3 else jnp.zeros_like(up)
                beside = jnp.where(lane == 0, before, up) + jnp.where(lane == 127, after, down)
                beside = beside + xs[q, part, b] + xs[q + 2, part, b]
                half = slice(part * 16, part * 16 + 16)
                beside = beside + xh[q, 0, b, half].astype(F32) + xh[q, 1, b, half].astype(F32)
                cross = s_im * x[1] if part == 0 else -(s_im * x[0])
                value = s_re * x[part] + cross - beside
                res[q, part, pl.ds(b, 16, stride=4), :] = source(q, part, b) - value
        return carry

    lax.fori_loop(0, 4, residual, 0)

    @pl.when(first & has_late)
    def _():
        for j in range(CUTS):
            late_copy(0, l, j).wait_send()

    @pl.when(first)
    def _():
        early_copy(0, l).wait_send()

    @pl.when(jnp.logical_not(first))
    def _():
        source_copy().wait_send()
        layer_copy(-1).wait_send()

    @pl.when(jnp.logical_not(last))
    def _():
        own_copy().wait_send()
        layer_copy(1).wait_send()

    @pl.when(at_turn)
    def _():
        for copy in turn_copies():
            copy.wait_send()

    @pl.when(on_route)
    def _():
        for k in range(ROUTED):
            route_copy(k, dense).wait_send()

    @pl.when(paired & (far_left & (w == 1) | far_right & (w == TURN - 2)))
    def _():
        far_copy(2, 2, l).wait_send()

    @pl.when(jnp.logical_not(last) & (l + 1 >= PAIRED) & (far_left & (w == 1) | far_right & (w == TURN - 2)))
    def _():
        far_copy(4, 2, l).wait_send()

    def drain(q, carry):
        @pl.when(has_left)
        def _():
            x_copy(q, -1).wait_send()

        @pl.when(has_right)
        def _():
            x_copy(q, 1).wait_send()

        handing = (q == 3) & jnp.logical_not(last)

        @pl.when((handing & has_late) | ((q < 3) & late_moves(q + 1)))
        def _():
            for j in range(CUTS):
                late_copy(q + 1, l, j).wait_send()

        @pl.when((q < 3) | handing)
        def _():
            early_copy(q + 1, l).wait_send()

        return carry

    lax.fori_loop(0, 4, drain, 0)


def write_results(sol, res, sol_out, res_out, sem):
    copies = [
        pltpu.make_async_copy(sol, sol_out, sem.at[0]),
        pltpu.make_async_copy(res, res_out, sem.at[1]),
    ]
    for copy in copies:
        copy.start()
    for copy in copies:
        copy.wait()


def per_device(layers, tiles, source_field, wave_shift, frontal_blocks, block_columns):
    field = pltpu.VMEM((4, 2, 64, 128), F32)
    hbm = pl.BlockSpec(memory_space=pltpu.HBM)
    dma = pltpu.SemaphoreType.DMA
    sol, res = pl.pallas_call(
        functools.partial(kernel, layers, tiles),
        out_shape=(field, field),
        in_specs=[hbm, hbm, hbm, hbm],
        out_specs=(pl.BlockSpec(memory_space=pltpu.VMEM),) * 2,
        scratch_shapes=[
            pltpu.VMEM((5, 2, 64, 128), F32),
            pltpu.VMEM((4, 8, 128), F32),
            pltpu.VMEM((4, 8, 2, 128, 128), BF16),
            pltpu.SMEM((4, 8), jnp.int32),
            pltpu.VMEM((4, 1152, 256), BF16),
            pltpu.VMEM((4, 1152, 256), BF16),
            pltpu.VMEM((2, 2, 64, 128), F32),
            pltpu.VMEM((5, 20, 32, 128), BF16),
            pltpu.VMEM((4, 4, 32, 128), BF16),
            pltpu.VMEM((4, 2, 4, 32, 128), BF16),
            pltpu.VMEM((2, 4, 32, 128), BF16),
            pltpu.VMEM((6, 2, 4, 16, 128), F32),
            pltpu.VMEM((4, 32, 256), F32),
            pltpu.VMEM((4, 32, 256), F32),
            dma((7,)),
            dma((5, CUTS)),
            dma((4, CUTS)),
            dma((5,)),
            dma((4,)),
            dma((5,)),
            dma((4,)),
            dma((4, 2)),
            dma((4, 2)),
            dma((4,)),
            dma((4,)),
            dma((4,)),
            dma((4,)),
            dma((ROUTED,)),
            dma((ROUTED,)),
        ],
        compiler_params=pltpu.CompilerParams(
            collective_id=0, has_side_effects=True, vmem_limit_bytes=32 * 1024 * 1024
        ),
    )(
        *[
            pltpu.with_memory_space_constraint(operand, pltpu.HBM)
            for operand in (
                source_field.reshape(4, 2, 64, 128),
                wave_shift.reshape(4, 8, 128),
                frontal_blocks[0],
                block_columns[0],
            )
        ]
    )
    whole = jax.ShapeDtypeStruct((4, 2, 64, 128), F32)
    out = pl.BlockSpec(memory_space=pltpu.HBM)
    sol, res = pl.pallas_call(
        write_results,
        out_shape=(whole, whole),
        in_specs=[pl.BlockSpec(memory_space=pltpu.VMEM)] * 2,
        out_specs=(out, out),
        scratch_shapes=[dma((2,))],
        compiler_params=pltpu.CompilerParams(vmem_limit_bytes=8 * 1024 * 1024),
    )(*[pltpu.with_memory_space_constraint(result, pltpu.VMEM) for result in (sol, res)])
    return sol.reshape(4, 2, 16, 1, 512), res.reshape(4, 2, 16, 1, 512)


def solution(mesh):
    placed = (
        P("layer", None, None, "tile", None),
        P("layer", None, "tile", None),
        P("layer", "tile", None, None, None, None),
        P("layer", "tile", None),
    )
    return jax.shard_map(
        functools.partial(per_device, mesh.shape["layer"], mesh.shape["tile"]),
        mesh=mesh,
        in_specs=placed,
        out_specs=(P("layer", None, None, "tile", None), P("layer", None, None, "tile", None)),
        check_vma=False,
    )
```

```python
import functools

import jax
import jax.numpy as jnp
from jax import lax
from jax.experimental import pallas as pl
from jax.experimental.pallas import tpu as pltpu
from jax.sharding import PartitionSpec as P

MESH = pl.DeviceIdType.MESH
F32, BF16 = jnp.float32, jnp.bfloat16
NB = 4
TURN = 8
PAIRED = 1
ROUTE = {7: (-2, -3), 4: (3, 6), 2: (-6, -2), 0: (2, 3), 3: (-3, -6), 5: (6, 2)}
ROUTED = 6
SPAN = 288
FAR_LEFT, LEFT, OWN, RIGHT, FAR_RIGHT = 0, 4, 8, 12, 16
REMOTE = 5


def places(v):
    return list(range(v, 4)) + list(range(8, 9 + v)) + [4, 5, 6, 7]


def kernel(
    layers, tiles, src, shift, fro, columns, sol, res,
    s_v, sh_v, fro_v, col, dense, other, s_other, ext, xo, xh, xlay, xs, acc, other_acc,
    lsem, lsend, lrecv, esend, erecv, fsend, frecv, xsend, xrecv, csend, crecv, gsend, grecv, rsend, rrecv,
):
    l, t = lax.axis_index("layer"), lax.axis_index("tile")
    first, last = l == 0, l == layers - 1
    has_left, has_right = t > 0, t < tiles - 1
    w = lax.rem(t, TURN)
    plain = lax.rem(t, 2) == 0
    where_is = [jnp.where(plain, p, 19 - p) for p in range(16)]
    row_of = [jnp.where(plain, b, 3 - b) for b in range(NB)]
    late = jnp.where(plain, -1, 1)
    has_late = jnp.where(plain, t, tiles - 1 - t) > 0
    turn_left, turn_right = has_left & (w == 0), has_right & (w == TURN - 1)
    far_left = (t > 1) & (w <= 1)
    far_right = (t < tiles - 2) & (w >= TURN - 2)
    far = jnp.where(far_right, 2, -2)
    paired = l >= PAIRED
    onto_next = (w == 7) | (w == 4) | (w == 5)
    on_route = paired & ((onto_next & (t < tiles - TURN)) | (((w == 0) | (w == 2) | (w == 3)) & (t >= TURN)))
    route_from = t + sum(jnp.where(w == place, ROUTE[place][0], 0) for place in ROUTE)
    route_to = t + sum(jnp.where(w == place, ROUTE[place][1], 0) for place in ROUTE)

    barrier = pltpu.get_barrier_semaphore()
    for there, dl, dt in (
        (has_left, 0, -1),
        (has_right, 0, 1),
        (paired & (far_left | far_right), 0, far),
        (jnp.logical_not(first), -1, 0),
        (jnp.logical_not(last), 1, 0),
    ):
        @pl.when(there)
        def _():
            pl.semaphore_signal(barrier, inc=1, device_id=(l + dl, t + dt), device_id_type=MESH)

    @pl.when(on_route)
    def _():
        for there in (route_from, route_to):
            pl.semaphore_signal(barrier, inc=1, device_id=(l, there), device_id_type=MESH)

    load_c = pltpu.make_async_copy(columns, col, lsem.at[0])
    load_s = pltpu.make_async_copy(src, s_v.at[pl.ds(0, 4)], lsem.at[1])
    load_w = pltpu.make_async_copy(shift, sh_v, lsem.at[2])
    load_f = [pltpu.make_async_copy(fro.at[row_of[v]], fro_v.at[v], lsem.at[3 + v]) for v in range(NB)]
    load_c.start()
    load_f[0].start()
    load_s.start()
    for b in range(1, NB):
        load_f[b].start()
    load_w.start()

    @pl.when(jnp.logical_not(has_left))
    def _():
        ext[:, LEFT : LEFT + 4] = jnp.zeros((5, 4, 32, 128), BF16)
        xh[:, 0] = jnp.zeros((4, 4, 32, 128), BF16)

    @pl.when(jnp.logical_not(has_right))
    def _():
        ext[:, RIGHT : RIGHT + 4] = jnp.zeros((5, 4, 32, 128), BF16)
        xh[:, 1] = jnp.zeros((4, 4, 32, 128), BF16)

    @pl.when(first)
    def _():
        xlay[0] = jnp.zeros((4, 32, 128), BF16)

    @pl.when(last)
    def _():
        xlay[1] = jnp.zeros((4, 32, 128), BF16)
        s_v[4] = jnp.zeros((2, 64, 128), F32)

    def source(q, part, b):
        return s_v[q, part, pl.ds(b, 16, stride=4), :]

    load_c.wait()
    for v in range(NB):
        load_f[v].wait()
        hit = [
            [col[row_of[v], k] == jnp.where(plain, c - v, 8 + v - c) for k in range(8)] for c in places(v)
        ]

        def densify(i, carry, v=v, hit=hit):
            r = pl.multiple_of(i * 16, 16)
            for part in range(2):
                blocks = [fro_v[v, k, part, pl.ds(r, 16), :].astype(F32) for k in range(8)]
                for place in range(9):
                    total = jnp.where(hit[place][0], blocks[0], 0.0)
                    for k in range(1, 8):
                        total = total + jnp.where(hit[place][k], blocks[k], 0.0)
                    dense[v, pl.ds(pl.multiple_of(place * 128 + r, 16), 16), part * 128 : part * 128 + 128] = total.astype(BF16)
            return carry

        lax.fori_loop(0, 8, densify, 0)

    load_s.wait()

    @pl.when(first)
    def _():
        for b in range(NB):
            ext[0, OWN + b, 0:16] = source(0, 0, b).astype(BF16)
            ext[0, OWN + b, 16:32] = source(0, 1, b).astype(BF16)

    one = lambda there: jnp.where(there, 1, 0)
    pl.semaphore_wait(
        barrier,
        one(has_left) + one(has_right) + one(paired & (far_left | far_right))
        + one(jnp.logical_not(first)) + one(jnp.logical_not(last)) + 2 * one(on_route),
    )

    def late_copy(q, to):
        return pltpu.make_async_remote_copy(
            src_ref=ext.at[q, pl.ds(OWN, 4)],
            dst_ref=ext.at[lax.rem(q, 4), pl.ds(jnp.where(plain, RIGHT, LEFT), 4)],
            send_sem=lsend.at[q],
            recv_sem=lrecv.at[lax.rem(q, 4)],
            device_id=(to, t + late),
            device_id_type=MESH,
        )

    def early_copy(q, to):
        return pltpu.make_async_remote_copy(
            src_ref=ext.at[q, pl.ds(OWN, 4)],
            dst_ref=ext.at[lax.rem(q, 4), pl.ds(jnp.where(plain, LEFT, RIGHT), 4)],
            send_sem=esend.at[q],
            recv_sem=erecv.at[lax.rem(q, 4)],
            device_id=(to, t - late),
            device_id_type=MESH,
        )

    def own_copy():
        return pltpu.make_async_remote_copy(
            src_ref=ext.at[4, pl.ds(OWN, 4)],
            dst_ref=ext.at[0, pl.ds(OWN, 4)],
            send_sem=csend.at[3],
            recv_sem=crecv.at[3],
            device_id=(l + 1, t),
            device_id_type=MESH,
        )

    def far_copy(q, dt, to):
        return pltpu.make_async_remote_copy(
            src_ref=ext.at[q, pl.ds(OWN, 4)],
            dst_ref=ext.at[lax.rem(q, 4), pl.ds(FAR_LEFT if dt == 2 else FAR_RIGHT, 4)],
            send_sem=fsend.at[q],
            recv_sem=frecv.at[lax.rem(q, 4)],
            device_id=(to, t + dt),
            device_id_type=MESH,
        )

    def x_copy(q, dt):
        side = (1 - dt) // 2
        return pltpu.make_async_remote_copy(
            src_ref=xo.at[q],
            dst_ref=xh.at[q, side],
            send_sem=xsend.at[q, side],
            recv_sem=xrecv.at[q, side],
            device_id=(l, t + dt),
            device_id_type=MESH,
        )

    def layer_copy(dl):
        side = (1 - dl) // 2
        return pltpu.make_async_remote_copy(
            src_ref=xo.at[3 if dl == 1 else 0],
            dst_ref=xlay.at[side],
            send_sem=csend.at[side],
            recv_sem=crecv.at[side],
            device_id=(l + dl, t),
            device_id_type=MESH,
        )

    def source_copy():
        return pltpu.make_async_remote_copy(
            src_ref=s_v.at[0],
            dst_ref=s_v.at[4],
            send_sem=csend.at[2],
            recv_sem=crecv.at[2],
            device_id=(l - 1, t),
            device_id_type=MESH,
        )

    across = t + jnp.where(turn_left, -1, 1)

    def turn_copies():
        rest = pl.ds(0, (16 - ROUTED) % 4 * SPAN)
        whole = pl.ds(0, (16 - ROUTED) // 4)
        pieces = [
            (dense.at[(16 - ROUTED) // 4, rest], other.at[(16 - ROUTED) // 4, rest]),
            (dense.at[whole], other.at[whole]),
            (s_v.at[1], s_other.at[0]),
            (s_v.at[3], s_other.at[1]),
        ]
        return [
            pltpu.make_async_remote_copy(
                src_ref=here,
                dst_ref=there,
                send_sem=gsend.at[i],
                recv_sem=grecv.at[i],
                device_id=(l, across),
                device_id_type=MESH,
            )
            for i, (here, there) in enumerate(pieces)
        ]

    at_turn = paired & (turn_left | turn_right)

    def route_copy(k, here):
        i = 15 - k
        piece = (i // 4, pl.ds(i % 4 * SPAN, SPAN))
        return pltpu.make_async_remote_copy(
            src_ref=here.at[piece],
            dst_ref=other.at[piece],
            send_sem=rsend.at[k],
            recv_sem=rrecv.at[k],
            device_id=(l, route_to),
            device_id_type=MESH,
        )

    def x_moves(q, dt):
        there, turn = (has_left, turn_left) if dt == -1 else (has_right, turn_right)
        return there & jnp.logical_not(paired & last & turn & (q == 3))

    def late_moves(q):
        return has_late & jnp.logical_not(at_turn & (lax.rem(q, 2) == 1))

    @pl.when(first & has_late)
    def _():
        late_copy(0, l).start()

    @pl.when(first)
    def _():
        early_copy(0, l).start()

    @pl.when(jnp.logical_not(first))
    def _():
        source_copy().start()

    @pl.when(at_turn)
    def _():
        for copy in turn_copies()[:1:-1]:
            copy.start()
        for k in range(ROUTED):
            route_copy(k, dense).start()
        for copy in turn_copies()[1::-1]:
            copy.start()

    @pl.when(on_route & jnp.logical_not(at_turn))
    def _():
        for k in range(ROUTED):
            route_copy(k, other).wait_recv()
            route_copy(k, other).start()

    def product(q, blocks, matrix, v, start):
        operand = jnp.concatenate([ext[q, where_is[p]] for p in blocks], axis=1)
        return jnp.dot(
            operand,
            matrix[v, start * 128 : (start + len(blocks)) * 128],
            preferred_element_type=F32,
        )

    def combine(total):
        re = total[0:16, 0:128] - total[16:32, 128:256]
        im = total[0:16, 128:256] + total[16:32, 0:128]
        return re, im

    def publish(q):
        for b in range(NB):
            for part in range(2):
                xo[q, b, part * 16 : part * 16 + 16] = xs[q + 1, part, b].astype(BF16)

        @pl.when(x_moves(q, -1))
        def _():
            x_copy(q, -1).start()

        @pl.when(x_moves(q, 1))
        def _():
            x_copy(q, 1).start()

        @pl.when((q == 0) & jnp.logical_not(first))
        def _():
            layer_copy(-1).start()

        @pl.when((q == 3) & jnp.logical_not(last))
        def _():
            layer_copy(1).start()

        for b in range(NB):
            for part in range(2):
                sol[q, part, pl.ds(b, 16, stride=4), :] = xs[q + 1, part, b]

    def others_late(q):
        for v in range(NB):
            other_acc[v] = product(q, [11 - c for c in places(v)[: 4 - v]], other, v, 0)

    def others_rest(q):
        for v in range(NB):
            other_acc[v] += product(q, [11 - c for c in places(v)[REMOTE:]], other, v, REMOTE)
        far_copy(q, 2, l).wait_recv()
        for v in range(NB):
            other_acc[v] += product(q, [11 - c for c in places(v)[4 - v : REMOTE]], other, v, 4 - v)

    def plane(q, carry):
        @pl.when(jnp.logical_not(first) & (q == 0))
        def _():
            own_copy().wait_recv()

        behind = at_turn & (lax.rem(q, 2) == 1)

        def begin(q):
            early_copy(q, l).wait_recv()
            for v in range(NB):
                acc[v] = product(q, [4 + c for c in places(v)[4 - v :]], dense, v, 4 - v)

        @pl.when(jnp.logical_not(behind))
        def _():
            begin(q)

        doubles = at_turn & (lax.rem(q, 2) == 0)

        @pl.when(doubles)
        def _():
            @pl.when(q == 0)
            def _():
                for copy in turn_copies():
                    copy.wait_recv()
                for k in range(ROUTED):
                    route_copy(k, dense).wait_recv()

            others_late(q)

        @pl.when((q == 3) & jnp.logical_not(last))
        def _():
            source_copy().wait_recv()

        def finish(v):
            b = row_of[v]
            re, im = combine(acc[v])
            ext[q + 1, OWN + b, 0:16] = (s_v[q + 1, 0, pl.ds(b, 16, stride=4), :] + re).astype(BF16)
            ext[q + 1, OWN + b, 16:32] = (s_v[q + 1, 1, pl.ds(b, 16, stride=4), :] + im).astype(BF16)
            xs[q + 1, 0, b] = re
            xs[q + 1, 1, b] = im

        @pl.when(late_moves(q))
        def _():
            late_copy(q, l).wait_recv()

        totals = [acc[v] + product(q, [4 + c for c in places(v)[: 4 - v]], dense, v, 0) for v in range(NB)]
        for v in range(NB):
            b = row_of[v]
            re, im = combine(totals[v])
            ext[q + 1, OWN + b, 0:16] = (s_v[q + 1, 0, pl.ds(b, 16, stride=4), :] + re).astype(BF16)
            ext[q + 1, OWN + b, 16:32] = (s_v[q + 1, 1, pl.ds(b, 16, stride=4), :] + im).astype(BF16)
            xs[q + 1, 0, b] = re
            xs[q + 1, 1, b] = im

        handing = (q == 3) & jnp.logical_not(last)
        onward = (q < 3) | jnp.logical_not(last)
        to = l + q // 3

        @pl.when((handing & has_late) | ((q < 3) & late_moves(q + 1)))
        def _():
            late_copy(q + 1, to).start()

        @pl.when(onward)
        def _():
            early_copy(q + 1, to).start()

        @pl.when(handing)
        def _():
            own_copy().start()

        sends_far = (handing & (l + 1 >= PAIRED)) | ((q == 1) & paired) | ((q == 2) & paired & last)

        @pl.when(sends_far & far_left & (w == 1))
        def _():
            far_copy(q + 1, -2, to).start()

        @pl.when(sends_far & far_right & (w == TURN - 2))
        def _():
            far_copy(q + 1, 2, to).start()

        @pl.when(doubles)
        def _():
            begin(q + 1)
            others_rest(q)
            into = jnp.where(turn_left, LEFT, RIGHT)
            for b in range(NB):
                re, im = combine(other_acc[3 - row_of[b]])
                there = [s_other[q // 2, part, pl.ds(b, 16, stride=4), :] for part in range(2)]
                ext[q + 1, into + b, 0:16] = (there[0] + re).astype(BF16)
                ext[q + 1, into + b, 16:32] = (there[1] + im).astype(BF16)

        @pl.when(lax.rem(q, 2) == 1)
        def _():
            publish(q)
            publish(q - 1)

        @pl.when(at_turn & last & (q == 3))
        def _():
            others_late(q)
            others_rest(q)
            for b in range(NB):
                re, im = combine(other_acc[3 - row_of[b]])
                xh[3, jnp.where(turn_left, 0, 1), b, 0:16] = re.astype(BF16)
                xh[3, jnp.where(turn_left, 0, 1), b, 16:32] = im.astype(BF16)

        return carry

    lax.fori_loop(0, 4, plane, 0)

    load_w.wait()

    @pl.when(jnp.logical_not(first))
    def _():
        layer_copy(1).wait_recv()

    @pl.when(jnp.logical_not(last))
    def _():
        layer_copy(-1).wait_recv()

    for b in range(NB):
        for part in range(2):
            xs[0, part, b] = xlay[0, b, part * 16 : part * 16 + 16].astype(F32)
            xs[5, part, b] = xlay[1, b, part * 16 : part * 16 + 16].astype(F32)

    lane = lax.broadcasted_iota(jnp.int32, (16, 128), 1)

    def residual(q, carry):
        @pl.when(x_moves(q, -1))
        def _():
            x_copy(q, 1).wait_recv()

        @pl.when(x_moves(q, 1))
        def _():
            x_copy(q, -1).wait_recv()

        for b in range(NB):
            s_re = 6.0 - sh_v[q, pl.ds(b, 1), :]
            s_im = sh_v[q, pl.ds(4 + b, 1), :]
            x = [xs[q + 1, part, b] for part in range(2)]
            for part in range(2):
                up = pltpu.roll(x[part], 1, 1)
                before = pltpu.roll(xs[q + 1, part, b - 1], 1, 1) if b > 0 else jnp.zeros_like(up)
                down = pltpu.roll(x[part], 127, 1)
                after = pltpu.roll(xs[q + 1, part, b + 1], 127, 1) if b < 3 else jnp.zeros_like(up)
                beside = jnp.where(lane == 0, before, up) + jnp.where(lane == 127, after, down)
                beside = beside + xs[q, part, b] + xs[q + 2, part, b]
                half = slice(part * 16, part * 16 + 16)
                beside = beside + xh[q, 0, b, half].astype(F32) + xh[q, 1, b, half].astype(F32)
                cross = s_im * x[1] if part == 0 else -(s_im * x[0])
                value = s_re * x[part] + cross - beside
                res[q, part, pl.ds(b, 16, stride=4), :] = source(q, part, b) - value
        return carry

    lax.fori_loop(0, 4, residual, 0)

    @pl.when(first & has_late)
    def _():
        late_copy(0, l).wait_send()

    @pl.when(first)
    def _():
        early_copy(0, l).wait_send()

    @pl.when(jnp.logical_not(first))
    def _():
        source_copy().wait_send()
        layer_copy(-1).wait_send()

    @pl.when(jnp.logical_not(last))
    def _():
        own_copy().wait_send()
        layer_copy(1).wait_send()

    @pl.when(at_turn)
    def _():
        for copy in turn_copies():
            copy.wait_send()

    @pl.when(on_route)
    def _():
        for k in range(ROUTED):
            route_copy(k, dense).wait_send()

    @pl.when(paired & (far_left & (w == 1) | far_right & (w == TURN - 2)))
    def _():
        far_copy(2, 2, l).wait_send()

        @pl.when(last)
        def _():
            far_copy(3, 2, l).wait_send()

    @pl.when(jnp.logical_not(last) & (l + 1 >= PAIRED) & (far_left & (w == 1) | far_right & (w == TURN - 2)))
    def _():
        far_copy(4, 2, l).wait_send()

    def drain(q, carry):
        @pl.when(x_moves(q, -1))
        def _():
            x_copy(q, -1).wait_send()

        @pl.when(x_moves(q, 1))
        def _():
            x_copy(q, 1).wait_send()

        handing = (q == 3) & jnp.logical_not(last)

        @pl.when((handing & has_late) | ((q < 3) & late_moves(q + 1)))
        def _():
            late_copy(q + 1, l).wait_send()

        @pl.when((q < 3) | handing)
        def _():
            early_copy(q + 1, l).wait_send()

        return carry

    lax.fori_loop(0, 4, drain, 0)


def write_results(sol, res, sol_out, res_out, sem):
    copies = [
        pltpu.make_async_copy(sol, sol_out, sem.at[0]),
        pltpu.make_async_copy(res, res_out, sem.at[1]),
    ]
    for copy in copies:
        copy.start()
    for copy in copies:
        copy.wait()


def per_device(layers, tiles, source_field, wave_shift, frontal_blocks, block_columns):
    field = pltpu.VMEM((4, 2, 64, 128), F32)
    hbm = pl.BlockSpec(memory_space=pltpu.HBM)
    dma = pltpu.SemaphoreType.DMA
    sol, res = pl.pallas_call(
        functools.partial(kernel, layers, tiles),
        out_shape=(field, field),
        in_specs=[hbm, hbm, hbm, hbm],
        out_specs=(pl.BlockSpec(memory_space=pltpu.VMEM),) * 2,
        scratch_shapes=[
            pltpu.VMEM((5, 2, 64, 128), F32),
            pltpu.VMEM((4, 8, 128), F32),
            pltpu.VMEM((4, 8, 2, 128, 128), BF16),
            pltpu.SMEM((4, 8), jnp.int32),
            pltpu.VMEM((4, 1152, 256), BF16),
            pltpu.VMEM((4, 1152, 256), BF16),
            pltpu.VMEM((2, 2, 64, 128), F32),
            pltpu.VMEM((5, 20, 32, 128), BF16),
            pltpu.VMEM((4, 4, 32, 128), BF16),
            pltpu.VMEM((4, 2, 4, 32, 128), BF16),
            pltpu.VMEM((2, 4, 32, 128), BF16),
            pltpu.VMEM((6, 2, 4, 16, 128), F32),
            pltpu.VMEM((4, 32, 256), F32),
            pltpu.VMEM((4, 32, 256), F32),
            dma((7,)),
            dma((5,)),
            dma((4,)),
            dma((5,)),
            dma((4,)),
            dma((5,)),
            dma((4,)),
            dma((4, 2)),
            dma((4, 2)),
            dma((4,)),
            dma((4,)),
            dma((4,)),
            dma((4,)),
            dma((ROUTED,)),
            dma((ROUTED,)),
        ],
        compiler_params=pltpu.CompilerParams(
            collective_id=0, has_side_effects=True, vmem_limit_bytes=32 * 1024 * 1024
        ),
    )(
        *[
            pltpu.with_memory_space_constraint(operand, pltpu.HBM)
            for operand in (
                source_field.reshape(4, 2, 64, 128),
                wave_shift.reshape(4, 8, 128),
                frontal_blocks[0],
                block_columns[0],
            )
        ]
    )
    whole = jax.ShapeDtypeStruct((4, 2, 64, 128), F32)
    out = pl.BlockSpec(memory_space=pltpu.HBM)
    sol, res = pl.pallas_call(
        write_results,
        out_shape=(whole, whole),
        in_specs=[pl.BlockSpec(memory_space=pltpu.VMEM)] * 2,
        out_specs=(out, out),
        scratch_shapes=[dma((2,))],
        compiler_params=pltpu.CompilerParams(vmem_limit_bytes=8 * 1024 * 1024),
    )(*[pltpu.with_memory_space_constraint(result, pltpu.VMEM) for result in (sol, res)])
    return sol.reshape(4, 2, 16, 1, 512), res.reshape(4, 2, 16, 1, 512)


def solution(mesh):
    placed = (
        P("layer", None, None, "tile", None),
        P("layer", None, "tile", None),
        P("layer", "tile", None, None, None, None),
        P("layer", "tile", None),
    )
    return jax.shard_map(
        functools.partial(per_device, mesh.shape["layer"], mesh.shape["tile"]),
        mesh=mesh,
        in_specs=placed,
        out_specs=(P("layer", None, None, "tile", None), P("layer", None, None, "tile", None)),
        check_vma=False,
    )
```

```python
import functools

import jax
import jax.numpy as jnp
from jax import lax
from jax.experimental import pallas as pl
from jax.experimental.pallas import tpu as pltpu
from jax.sharding import PartitionSpec as P

MESH = pl.DeviceIdType.MESH
F32, BF16 = jnp.float32, jnp.bfloat16
NB = 4
TURN = 8
PAIRED = 1
ROUTE = {7: (-2, -3), 4: (3, 6), 2: (-6, -2), 0: (2, 3), 3: (-3, -6), 5: (6, 2)}
ROUTED = 6
SPAN = 288
FAR_LEFT, LEFT, OWN, RIGHT, FAR_RIGHT = 0, 4, 8, 12, 16
REMOTE = 5


def places(v):
    return list(range(v, 4)) + list(range(8, 9 + v)) + [4, 5, 6, 7]


def kernel(
    layers, tiles, src, shift, fro, columns, sol, res,
    s_v, sh_v, fro_v, col, dense, other, s_other, ext, xo, xh, xlay, xs, acc, other_acc,
    lsem, lsend, lrecv, esend, erecv, fsend, frecv, xsend, xrecv, csend, crecv, gsend, grecv, rsend, rrecv,
):
    l, t = lax.axis_index("layer"), lax.axis_index("tile")
    first, last = l == 0, l == layers - 1
    has_left, has_right = t > 0, t < tiles - 1
    w = lax.rem(t, TURN)
    plain = lax.rem(t, 2) == 0
    where_is = [jnp.where(plain, p, 19 - p) for p in range(16)]
    row_of = [jnp.where(plain, b, 3 - b) for b in range(NB)]
    late = jnp.where(plain, -1, 1)
    has_late = jnp.where(plain, t, tiles - 1 - t) > 0
    turn_left, turn_right = has_left & (w == 0), has_right & (w == TURN - 1)
    far_left = (t > 1) & (w <= 1)
    far_right = (t < tiles - 2) & (w >= TURN - 2)
    far = jnp.where(far_right, 2, -2)
    paired = l >= PAIRED
    onto_next = (w == 7) | (w == 4) | (w == 5)
    on_route = paired & ((onto_next & (t < tiles - TURN)) | (((w == 0) | (w == 2) | (w == 3)) & (t >= TURN)))
    route_from = t + sum(jnp.where(w == place, ROUTE[place][0], 0) for place in ROUTE)
    route_to = t + sum(jnp.where(w == place, ROUTE[place][1], 0) for place in ROUTE)

    barrier = pltpu.get_barrier_semaphore()
    for there, dl, dt in (
        (has_left, 0, -1),
        (has_right, 0, 1),
        (paired & (far_left | far_right), 0, far),
        (jnp.logical_not(first), -1, 0),
        (jnp.logical_not(last), 1, 0),
    ):
        @pl.when(there)
        def _():
            pl.semaphore_signal(barrier, inc=1, device_id=(l + dl, t + dt), device_id_type=MESH)

    @pl.when(on_route)
    def _():
        for there in (route_from, route_to):
            pl.semaphore_signal(barrier, inc=1, device_id=(l, there), device_id_type=MESH)

    load_c = pltpu.make_async_copy(columns, col, lsem.at[0])
    load_s = pltpu.make_async_copy(src, s_v.at[pl.ds(0, 4)], lsem.at[1])
    load_w = pltpu.make_async_copy(shift, sh_v, lsem.at[2])
    load_f = [pltpu.make_async_copy(fro.at[row_of[v]], fro_v.at[v], lsem.at[3 + v]) for v in range(NB)]
    load_c.start()
    load_f[0].start()
    load_s.start()
    for b in range(1, NB):
        load_f[b].start()
    load_w.start()

    @pl.when(jnp.logical_not(has_left))
    def _():
        ext[:, LEFT : LEFT + 4] = jnp.zeros((5, 4, 32, 128), BF16)
        xh[:, 0] = jnp.zeros((4, 4, 32, 128), BF16)

    @pl.when(jnp.logical_not(has_right))
    def _():
        ext[:, RIGHT : RIGHT + 4] = jnp.zeros((5, 4, 32, 128), BF16)
        xh[:, 1] = jnp.zeros((4, 4, 32, 128), BF16)

    @pl.when(first)
    def _():
        xlay[0] = jnp.zeros((4, 32, 128), BF16)

    @pl.when(last)
    def _():
        xlay[1] = jnp.zeros((4, 32, 128), BF16)
        s_v[4] = jnp.zeros((2, 64, 128), F32)

    def source(q, part, b):
        return s_v[q, part, pl.ds(b, 16, stride=4), :]

    load_c.wait()
    for v in range(NB):
        load_f[v].wait()
        hit = [
            [col[row_of[v], k] == jnp.where(plain, c - v, 8 + v - c) for k in range(8)] for c in places(v)
        ]

        def densify(i, carry, v=v, hit=hit):
            r = pl.multiple_of(i * 16, 16)
            for part in range(2):
                blocks = [fro_v[v, k, part, pl.ds(r, 16), :].astype(F32) for k in range(8)]
                for place in range(9):
                    total = jnp.where(hit[place][0], blocks[0], 0.0)
                    for k in range(1, 8):
                        total = total + jnp.where(hit[place][k], blocks[k], 0.0)
                    dense[v, pl.ds(pl.multiple_of(place * 128 + r, 16), 16), part * 128 : part * 128 + 128] = total.astype(BF16)
            return carry

        lax.fori_loop(0, 8, densify, 0)

    load_s.wait()

    @pl.when(first)
    def _():
        for b in range(NB):
            ext[0, OWN + b, 0:16] = source(0, 0, b).astype(BF16)
            ext[0, OWN + b, 16:32] = source(0, 1, b).astype(BF16)

    one = lambda there: jnp.where(there, 1, 0)
    pl.semaphore_wait(
        barrier,
        one(has_left) + one(has_right) + one(paired & (far_left | far_right))
        + one(jnp.logical_not(first)) + one(jnp.logical_not(last)) + 2 * one(on_route),
    )

    def late_copy(q, to):
        return pltpu.make_async_remote_copy(
            src_ref=ext.at[q, pl.ds(OWN, 4)],
            dst_ref=ext.at[lax.rem(q, 4), pl.ds(jnp.where(plain, RIGHT, LEFT), 4)],
            send_sem=lsend.at[q],
            recv_sem=lrecv.at[lax.rem(q, 4)],
            device_id=(to, t + late),
            device_id_type=MESH,
        )

    def early_copy(q, to):
        return pltpu.make_async_remote_copy(
            src_ref=ext.at[q, pl.ds(OWN, 4)],
            dst_ref=ext.at[lax.rem(q, 4), pl.ds(jnp.where(plain, LEFT, RIGHT), 4)],
            send_sem=esend.at[q],
            recv_sem=erecv.at[lax.rem(q, 4)],
            device_id=(to, t - late),
            device_id_type=MESH,
        )

    def own_copy():
        return pltpu.make_async_remote_copy(
            src_ref=ext.at[4, pl.ds(OWN, 4)],
            dst_ref=ext.at[0, pl.ds(OWN, 4)],
            send_sem=csend.at[3],
            recv_sem=crecv.at[3],
            device_id=(l + 1, t),
            device_id_type=MESH,
        )

    def far_copy(q, dt, to):
        return pltpu.make_async_remote_copy(
            src_ref=ext.at[q, pl.ds(OWN, 4)],
            dst_ref=ext.at[lax.rem(q, 4), pl.ds(FAR_LEFT if dt == 2 else FAR_RIGHT, 4)],
            send_sem=fsend.at[q],
            recv_sem=frecv.at[lax.rem(q, 4)],
            device_id=(to, t + dt),
            device_id_type=MESH,
        )

    def x_copy(q, dt):
        side = (1 - dt) // 2
        return pltpu.make_async_remote_copy(
            src_ref=xo.at[q],
            dst_ref=xh.at[q, side],
            send_sem=xsend.at[q, side],
            recv_sem=xrecv.at[q, side],
            device_id=(l, t + dt),
            device_id_type=MESH,
        )

    def layer_copy(dl):
        side = (1 - dl) // 2
        return pltpu.make_async_remote_copy(
            src_ref=xo.at[3 if dl == 1 else 0],
            dst_ref=xlay.at[side],
            send_sem=csend.at[side],
            recv_sem=crecv.at[side],
            device_id=(l + dl, t),
            device_id_type=MESH,
        )

    def source_copy():
        return pltpu.make_async_remote_copy(
            src_ref=s_v.at[0],
            dst_ref=s_v.at[4],
            send_sem=csend.at[2],
            recv_sem=crecv.at[2],
            device_id=(l - 1, t),
            device_id_type=MESH,
        )

    across = t + jnp.where(turn_left, -1, 1)

    def turn_copies():
        rest = pl.ds(0, (16 - ROUTED) % 4 * SPAN)
        whole = pl.ds(0, (16 - ROUTED) // 4)
        pieces = [
            (dense.at[(16 - ROUTED) // 4, rest], other.at[(16 - ROUTED) // 4, rest]),
            (dense.at[whole], other.at[whole]),
            (s_v.at[1], s_other.at[0]),
            (s_v.at[3], s_other.at[1]),
        ]
        return [
            pltpu.make_async_remote_copy(
                src_ref=here,
                dst_ref=there,
                send_sem=gsend.at[i],
                recv_sem=grecv.at[i],
                device_id=(l, across),
                device_id_type=MESH,
            )
            for i, (here, there) in enumerate(pieces)
        ]

    at_turn = paired & (turn_left | turn_right)

    def route_copy(k, here):
        i = 15 - k
        piece = (i // 4, pl.ds(i % 4 * SPAN, SPAN))
        return pltpu.make_async_remote_copy(
            src_ref=here.at[piece],
            dst_ref=other.at[piece],
            send_sem=rsend.at[k],
            recv_sem=rrecv.at[k],
            device_id=(l, route_to),
            device_id_type=MESH,
        )

    def x_moves(q, dt):
        there, turn = (has_left, turn_left) if dt == -1 else (has_right, turn_right)
        return there & jnp.logical_not(paired & last & turn & (q == 3))

    def late_moves(q):
        return has_late & jnp.logical_not(at_turn & (lax.rem(q, 2) == 1))

    @pl.when(first & has_late)
    def _():
        late_copy(0, l).start()

    @pl.when(first)
    def _():
        early_copy(0, l).start()

    @pl.when(jnp.logical_not(first))
    def _():
        source_copy().start()

    @pl.when(at_turn)
    def _():
        for copy in turn_copies()[:1:-1]:
            copy.start()
        for k in range(ROUTED):
            route_copy(k, dense).start()
        for copy in turn_copies()[1::-1]:
            copy.start()

    @pl.when(on_route & jnp.logical_not(at_turn))
    def _():
        for k in range(ROUTED):
            route_copy(k, other).wait_recv()
            route_copy(k, other).start()

    def product(q, blocks, matrix, v, start):
        operand = jnp.concatenate([ext[q, where_is[p]] for p in blocks], axis=1)
        return jnp.dot(
            operand,
            matrix[v, start * 128 : (start + len(blocks)) * 128],
            preferred_element_type=F32,
        )

    def combine(total):
        re = total[0:16, 0:128] - total[16:32, 128:256]
        im = total[0:16, 128:256] + total[16:32, 0:128]
        return re, im

    def publish(q):
        for b in range(NB):
            for part in range(2):
                xo[q, b, part * 16 : part * 16 + 16] = xs[q + 1, part, b].astype(BF16)

        @pl.when(x_moves(q, -1))
        def _():
            x_copy(q, -1).start()

        @pl.when(x_moves(q, 1))
        def _():
            x_copy(q, 1).start()

        @pl.when((q == 0) & jnp.logical_not(first))
        def _():
            layer_copy(-1).start()

        @pl.when((q == 3) & jnp.logical_not(last))
        def _():
            layer_copy(1).start()

        for b in range(NB):
            for part in range(2):
                sol[q, part, pl.ds(b, 16, stride=4), :] = xs[q + 1, part, b]

    def others_late(q):
        for v in range(NB):
            other_acc[v] = product(q, [11 - c for c in places(v)[: 4 - v]], other, v, 0)

    def others_rest(q):
        for v in range(NB):
            other_acc[v] += product(q, [11 - c for c in places(v)[REMOTE:]], other, v, REMOTE)
        far_copy(q, 2, l).wait_recv()
        for v in range(NB):
            other_acc[v] += product(q, [11 - c for c in places(v)[4 - v : REMOTE]], other, v, 4 - v)

    def plane(q, carry):
        @pl.when(jnp.logical_not(first) & (q == 0))
        def _():
            own_copy().wait_recv()

        behind = at_turn & (lax.rem(q, 2) == 1)

        def begin(q):
            early_copy(q, l).wait_recv()
            for v in range(NB):
                acc[v] = product(q, [4 + c for c in places(v)[4 - v :]], dense, v, 4 - v)

        @pl.when(jnp.logical_not(behind))
        def _():
            begin(q)

        doubles = at_turn & (lax.rem(q, 2) == 0)

        @pl.when(doubles)
        def _():
            @pl.when(q == 0)
            def _():
                for copy in turn_copies():
                    copy.wait_recv()
                for k in range(ROUTED):
                    route_copy(k, dense).wait_recv()

            others_late(q)

        @pl.when((q == 3) & jnp.logical_not(last))
        def _():
            source_copy().wait_recv()

        def finish(v):
            b = row_of[v]
            re, im = combine(acc[v])
            ext[q + 1, OWN + b, 0:16] = (s_v[q + 1, 0, pl.ds(b, 16, stride=4), :] + re).astype(BF16)
            ext[q + 1, OWN + b, 16:32] = (s_v[q + 1, 1, pl.ds(b, 16, stride=4), :] + im).astype(BF16)
            xs[q + 1, 0, b] = re
            xs[q + 1, 1, b] = im

        @pl.when(late_moves(q))
        def _():
            late_copy(q, l).wait_recv()

        totals = [acc[v] + product(q, [4 + c for c in places(v)[: 4 - v]], dense, v, 0) for v in range(NB)]
        for v in range(NB):
            b = row_of[v]
            re, im = combine(totals[v])
            ext[q + 1, OWN + b, 0:16] = (s_v[q + 1, 0, pl.ds(b, 16, stride=4), :] + re).astype(BF16)
            ext[q + 1, OWN + b, 16:32] = (s_v[q + 1, 1, pl.ds(b, 16, stride=4), :] + im).astype(BF16)
            xs[q + 1, 0, b] = re
            xs[q + 1, 1, b] = im

        handing = (q == 3) & jnp.logical_not(last)
        onward = (q < 3) | jnp.logical_not(last)
        to = l + q // 3

        @pl.when((handing & has_late) | ((q < 3) & late_moves(q + 1)))
        def _():
            late_copy(q + 1, to).start()

        @pl.when(onward)
        def _():
            early_copy(q + 1, to).start()

        @pl.when(handing)
        def _():
            own_copy().start()

        sends_far = (handing & (l + 1 >= PAIRED)) | ((q == 1) & paired) | ((q == 2) & paired & last)

        @pl.when(sends_far & far_left & (w == 1))
        def _():
            far_copy(q + 1, -2, to).start()

        @pl.when(sends_far & far_right & (w == TURN - 2))
        def _():
            far_copy(q + 1, 2, to).start()

        @pl.when(doubles)
        def _():
            begin(q + 1)
            others_rest(q)
            into = jnp.where(turn_left, LEFT, RIGHT)
            for b in range(NB):
                re, im = combine(other_acc[3 - row_of[b]])
                there = [s_other[q // 2, part, pl.ds(b, 16, stride=4), :] for part in range(2)]
                ext[q + 1, into + b, 0:16] = (there[0] + re).astype(BF16)
                ext[q + 1, into + b, 16:32] = (there[1] + im).astype(BF16)

        @pl.when(lax.rem(q, 2) == 1)
        def _():
            publish(q)
            publish(q - 1)

        @pl.when(at_turn & last & (q == 3))
        def _():
            others_late(q)
            others_rest(q)
            for b in range(NB):
                re, im = combine(other_acc[3 - row_of[b]])
                xh[3, jnp.where(turn_left, 0, 1), b, 0:16] = re.astype(BF16)
                xh[3, jnp.where(turn_left, 0, 1), b, 16:32] = im.astype(BF16)

        return carry

    for q in range(4):
        plane(q, 0)

    load_w.wait()

    @pl.when(jnp.logical_not(first))
    def _():
        layer_copy(1).wait_recv()

    @pl.when(jnp.logical_not(last))
    def _():
        layer_copy(-1).wait_recv()

    for b in range(NB):
        for part in range(2):
            xs[0, part, b] = xlay[0, b, part * 16 : part * 16 + 16].astype(F32)
            xs[5, part, b] = xlay[1, b, part * 16 : part * 16 + 16].astype(F32)

    lane = lax.broadcasted_iota(jnp.int32, (16, 128), 1)

    def residual(q, carry):
        @pl.when(x_moves(q, -1))
        def _():
            x_copy(q, 1).wait_recv()

        @pl.when(x_moves(q, 1))
        def _():
            x_copy(q, -1).wait_recv()

        for b in range(NB):
            s_re = 6.0 - sh_v[q, pl.ds(b, 1), :]
            s_im = sh_v[q, pl.ds(4 + b, 1), :]
            x = [xs[q + 1, part, b] for part in range(2)]
            for part in range(2):
                up = pltpu.roll(x[part], 1, 1)
                before = pltpu.roll(xs[q + 1, part, b - 1], 1, 1) if b > 0 else jnp.zeros_like(up)
                down = pltpu.roll(x[part], 127, 1)
                after = pltpu.roll(xs[q + 1, part, b + 1], 127, 1) if b < 3 else jnp.zeros_like(up)
                beside = jnp.where(lane == 0, before, up) + jnp.where(lane == 127, after, down)
                beside = beside + xs[q, part, b] + xs[q + 2, part, b]
                half = slice(part * 16, part * 16 + 16)
                beside = beside + xh[q, 0, b, half].astype(F32) + xh[q, 1, b, half].astype(F32)
                cross = s_im * x[1] if part == 0 else -(s_im * x[0])
                value = s_re * x[part] + cross - beside
                res[q, part, pl.ds(b, 16, stride=4), :] = source(q, part, b) - value
        return carry

    for q in range(4):
        residual(q, 0)

    @pl.when(first & has_late)
    def _():
        late_copy(0, l).wait_send()

    @pl.when(first)
    def _():
        early_copy(0, l).wait_send()

    @pl.when(jnp.logical_not(first))
    def _():
        source_copy().wait_send()
        layer_copy(-1).wait_send()

    @pl.when(jnp.logical_not(last))
    def _():
        own_copy().wait_send()
        layer_copy(1).wait_send()

    @pl.when(at_turn)
    def _():
        for copy in turn_copies():
            copy.wait_send()

    @pl.when(on_route)
    def _():
        for k in range(ROUTED):
            route_copy(k, dense).wait_send()

    @pl.when(paired & (far_left & (w == 1) | far_right & (w == TURN - 2)))
    def _():
        far_copy(2, 2, l).wait_send()

        @pl.when(last)
        def _():
            far_copy(3, 2, l).wait_send()

    @pl.when(jnp.logical_not(last) & (l + 1 >= PAIRED) & (far_left & (w == 1) | far_right & (w == TURN - 2)))
    def _():
        far_copy(4, 2, l).wait_send()

    def drain(q, carry):
        @pl.when(x_moves(q, -1))
        def _():
            x_copy(q, -1).wait_send()

        @pl.when(x_moves(q, 1))
        def _():
            x_copy(q, 1).wait_send()

        handing = (q == 3) & jnp.logical_not(last)

        @pl.when((handing & has_late) | ((q < 3) & late_moves(q + 1)))
        def _():
            late_copy(q + 1, l).wait_send()

        @pl.when((q < 3) | handing)
        def _():
            early_copy(q + 1, l).wait_send()

        return carry

    lax.fori_loop(0, 4, drain, 0)


def write_results(sol, res, sol_out, res_out, sem):
    copies = [
        pltpu.make_async_copy(here.at[q], there.at[q], sem.at[i, q])
        for q in range(4)
        for i, (here, there) in enumerate(((sol, sol_out), (res, res_out)))
    ]
    for copy in copies:
        copy.start()
    for copy in copies:
        copy.wait()


def per_device(layers, tiles, source_field, wave_shift, frontal_blocks, block_columns):
    field = pltpu.VMEM((4, 2, 64, 128), F32)
    hbm = pl.BlockSpec(memory_space=pltpu.HBM)
    dma = pltpu.SemaphoreType.DMA
    sol, res = pl.pallas_call(
        functools.partial(kernel, layers, tiles),
        out_shape=(field, field),
        in_specs=[hbm, hbm, hbm, hbm],
        out_specs=(pl.BlockSpec(memory_space=pltpu.VMEM),) * 2,
        scratch_shapes=[
            pltpu.VMEM((5, 2, 64, 128), F32),
            pltpu.VMEM((4, 8, 128), F32),
            pltpu.VMEM((4, 8, 2, 128, 128), BF16),
            pltpu.SMEM((4, 8), jnp.int32),
            pltpu.VMEM((4, 1152, 256), BF16),
            pltpu.VMEM((4, 1152, 256), BF16),
            pltpu.VMEM((2, 2, 64, 128), F32),
            pltpu.VMEM((5, 20, 32, 128), BF16),
            pltpu.VMEM((4, 4, 32, 128), BF16),
            pltpu.VMEM((4, 2, 4, 32, 128), BF16),
            pltpu.VMEM((2, 4, 32, 128), BF16),
            pltpu.VMEM((6, 2, 4, 16, 128), F32),
            pltpu.VMEM((4, 32, 256), F32),
            pltpu.VMEM((4, 32, 256), F32),
            dma((7,)),
            dma((5,)),
            dma((4,)),
            dma((5,)),
            dma((4,)),
            dma((5,)),
            dma((4,)),
            dma((4, 2)),
            dma((4, 2)),
            dma((4,)),
            dma((4,)),
            dma((4,)),
            dma((4,)),
            dma((ROUTED,)),
            dma((ROUTED,)),
        ],
        compiler_params=pltpu.CompilerParams(
            collective_id=0, has_side_effects=True, vmem_limit_bytes=32 * 1024 * 1024
        ),
    )(
        *[
            pltpu.with_memory_space_constraint(operand, pltpu.HBM)
            for operand in (
                source_field.reshape(4, 2, 64, 128),
                wave_shift.reshape(4, 8, 128),
                frontal_blocks[0],
                block_columns[0],
            )
        ]
    )
    whole = jax.ShapeDtypeStruct((4, 2, 64, 128), F32)
    out = pl.BlockSpec(memory_space=pltpu.HBM)
    sol, res = pl.pallas_call(
        write_results,
        out_shape=(whole, whole),
        in_specs=[pl.BlockSpec(memory_space=pltpu.VMEM)] * 2,
        out_specs=(out, out),
        scratch_shapes=[dma((2, 4))],
        compiler_params=pltpu.CompilerParams(vmem_limit_bytes=8 * 1024 * 1024),
    )(*[pltpu.with_memory_space_constraint(result, pltpu.VMEM) for result in (sol, res)])
    return sol.reshape(4, 2, 16, 1, 512), res.reshape(4, 2, 16, 1, 512)


def solution(mesh):
    placed = (
        P("layer", None, None, "tile", None),
        P("layer", None, "tile", None),
        P("layer", "tile", None, None, None, None),
        P("layer", "tile", None),
    )
    return jax.shard_map(
        functools.partial(per_device, mesh.shape["layer"], mesh.shape["tile"]),
        mesh=mesh,
        in_specs=placed,
        out_specs=(P("layer", None, None, "tile", None), P("layer", None, None, "tile", None)),
        check_vma=False,
    )
```

```python
import functools

import jax
import jax.numpy as jnp
from jax import lax
from jax.experimental import pallas as pl
from jax.experimental.pallas import tpu as pltpu
from jax.sharding import PartitionSpec as P

MESH = pl.DeviceIdType.MESH
F32, BF16 = jnp.float32, jnp.bfloat16
NB = 4
TURN = 8
PAIRED = 1
ROUTE = {7: (-2, -3), 4: (3, 6), 2: (-6, -2), 0: (2, 3), 3: (-3, -6), 5: (6, 2)}
ROUTED = 6
SPAN = 288
FAR_LEFT, LEFT, OWN, RIGHT, FAR_RIGHT = 0, 4, 8, 12, 16
REMOTE = 5


def places(v):
    return list(range(v, 4)) + list(range(8, 9 + v)) + [4, 5, 6, 7]


def kernel(
    layers, tiles, src, shift, fro, columns, sol, res,
    s_v, sh_v, fro_v, col, dense, other, s_other, ext, xo, xh, xlay, xs, acc, other_acc,
    lsem, lsend, lrecv, esend, erecv, fsend, frecv, xsend, xrecv, csend, crecv, gsend, grecv, rsend, rrecv,
):
    l, t = lax.axis_index("layer"), lax.axis_index("tile")
    first, last = l == 0, l == layers - 1
    has_left, has_right = t > 0, t < tiles - 1
    w = lax.rem(t, TURN)
    plain = lax.rem(t, 2) == 0
    where_is = [jnp.where(plain, p, 19 - p) for p in range(16)]
    row_of = [jnp.where(plain, b, 3 - b) for b in range(NB)]
    late = jnp.where(plain, -1, 1)
    has_late = jnp.where(plain, t, tiles - 1 - t) > 0
    turn_left, turn_right = has_left & (w == 0), has_right & (w == TURN - 1)
    far_left = (t > 1) & (w <= 1)
    far_right = (t < tiles - 2) & (w >= TURN - 2)
    far = jnp.where(far_right, 2, -2)
    paired = l >= PAIRED
    onto_next = (w == 7) | (w == 4) | (w == 5)
    on_route = paired & ((onto_next & (t < tiles - TURN)) | (((w == 0) | (w == 2) | (w == 3)) & (t >= TURN)))
    route_from = t + sum(jnp.where(w == place, ROUTE[place][0], 0) for place in ROUTE)
    route_to = t + sum(jnp.where(w == place, ROUTE[place][1], 0) for place in ROUTE)

    barrier = pltpu.get_barrier_semaphore()
    for there, dl, dt in (
        (has_left, 0, -1),
        (has_right, 0, 1),
        (paired & (far_left | far_right), 0, far),
        (jnp.logical_not(first), -1, 0),
        (jnp.logical_not(last), 1, 0),
    ):
        @pl.when(there)
        def _():
            pl.semaphore_signal(barrier, inc=1, device_id=(l + dl, t + dt), device_id_type=MESH)

    @pl.when(on_route)
    def _():
        for there in (route_from, route_to):
            pl.semaphore_signal(barrier, inc=1, device_id=(l, there), device_id_type=MESH)

    load_c = pltpu.make_async_copy(columns, col, lsem.at[0])
    load_s = pltpu.make_async_copy(src, s_v.at[pl.ds(0, 4)], lsem.at[1])
    load_w = pltpu.make_async_copy(shift, sh_v, lsem.at[2])
    load_f = [pltpu.make_async_copy(fro.at[row_of[v]], fro_v.at[v], lsem.at[3 + v]) for v in range(NB)]
    load_c.start()
    load_f[0].start()
    load_s.start()
    for b in range(1, NB):
        load_f[b].start()
    load_w.start()

    @pl.when(jnp.logical_not(has_left))
    def _():
        ext[:, LEFT : LEFT + 4] = jnp.zeros((5, 4, 32, 128), BF16)
        xh[:, 0] = jnp.zeros((4, 4, 32, 128), BF16)

    @pl.when(jnp.logical_not(has_right))
    def _():
        ext[:, RIGHT : RIGHT + 4] = jnp.zeros((5, 4, 32, 128), BF16)
        xh[:, 1] = jnp.zeros((4, 4, 32, 128), BF16)

    @pl.when(first)
    def _():
        xlay[0] = jnp.zeros((4, 32, 128), BF16)

    @pl.when(last)
    def _():
        xlay[1] = jnp.zeros((4, 32, 128), BF16)
        s_v[4] = jnp.zeros((2, 64, 128), F32)

    def source(q, part, b):
        return s_v[q, part, pl.ds(b, 16, stride=4), :]

    load_c.wait()
    for v in range(NB):
        load_f[v].wait()
        hit = [
            [col[row_of[v], k] == jnp.where(plain, c - v, 8 + v - c) for k in range(8)] for c in places(v)
        ]

        def densify(i, carry, v=v, hit=hit):
            r = pl.multiple_of(i * 16, 16)
            for part in range(2):
                blocks = [fro_v[v, k, part, pl.ds(r, 16), :].astype(F32) for k in range(8)]
                for place in range(9):
                    total = jnp.where(hit[place][0], blocks[0], 0.0)
                    for k in range(1, 8):
                        total = total + jnp.where(hit[place][k], blocks[k], 0.0)
                    dense[v, pl.ds(pl.multiple_of(place * 128 + r, 16), 16), part * 128 : part * 128 + 128] = total.astype(BF16)
            return carry

        lax.fori_loop(0, 8, densify, 0)

    load_s.wait()

    @pl.when(first)
    def _():
        for b in range(NB):
            ext[0, OWN + b, 0:16] = source(0, 0, b).astype(BF16)
            ext[0, OWN + b, 16:32] = source(0, 1, b).astype(BF16)

    one = lambda there: jnp.where(there, 1, 0)
    pl.semaphore_wait(
        barrier,
        one(has_left) + one(has_right) + one(paired & (far_left | far_right))
        + one(jnp.logical_not(first)) + one(jnp.logical_not(last)) + 2 * one(on_route),
    )

    def late_copy(q, to):
        return pltpu.make_async_remote_copy(
            src_ref=ext.at[q, pl.ds(OWN, 4)],
            dst_ref=ext.at[lax.rem(q, 4), pl.ds(jnp.where(plain, RIGHT, LEFT), 4)],
            send_sem=lsend.at[q],
            recv_sem=lrecv.at[lax.rem(q, 4)],
            device_id=(to, t + late),
            device_id_type=MESH,
        )

    def early_copy(q, to):
        return pltpu.make_async_remote_copy(
            src_ref=ext.at[q, pl.ds(OWN, 4)],
            dst_ref=ext.at[lax.rem(q, 4), pl.ds(jnp.where(plain, LEFT, RIGHT), 4)],
            send_sem=esend.at[q],
            recv_sem=erecv.at[lax.rem(q, 4)],
            device_id=(to, t - late),
            device_id_type=MESH,
        )

    def own_copy():
        return pltpu.make_async_remote_copy(
            src_ref=ext.at[4, pl.ds(OWN, 4)],
            dst_ref=ext.at[0, pl.ds(OWN, 4)],
            send_sem=csend.at[3],
            recv_sem=crecv.at[3],
            device_id=(l + 1, t),
            device_id_type=MESH,
        )

    def far_copy(q, dt, to):
        return pltpu.make_async_remote_copy(
            src_ref=ext.at[q, pl.ds(OWN, 4)],
            dst_ref=ext.at[lax.rem(q, 4), pl.ds(FAR_LEFT if dt == 2 else FAR_RIGHT, 4)],
            send_sem=fsend.at[q],
            recv_sem=frecv.at[lax.rem(q, 4)],
            device_id=(to, t + dt),
            device_id_type=MESH,
        )

    def x_copy(q, dt):
        side = (1 - dt) // 2
        return pltpu.make_async_remote_copy(
            src_ref=xo.at[q],
            dst_ref=xh.at[q, side],
            send_sem=xsend.at[q, side],
            recv_sem=xrecv.at[q, side],
            device_id=(l, t + dt),
            device_id_type=MESH,
        )

    def layer_copy(dl):
        side = (1 - dl) // 2
        return pltpu.make_async_remote_copy(
            src_ref=xo.at[3 if dl == 1 else 0],
            dst_ref=xlay.at[side],
            send_sem=csend.at[side],
            recv_sem=crecv.at[side],
            device_id=(l + dl, t),
            device_id_type=MESH,
        )

    def source_copy():
        return pltpu.make_async_remote_copy(
            src_ref=s_v.at[0],
            dst_ref=s_v.at[4],
            send_sem=csend.at[2],
            recv_sem=crecv.at[2],
            device_id=(l - 1, t),
            device_id_type=MESH,
        )

    across = t + jnp.where(turn_left, -1, 1)

    def turn_copies():
        rest = pl.ds(0, (16 - ROUTED) % 4 * SPAN)
        whole = pl.ds(0, (16 - ROUTED) // 4)
        pieces = [
            (dense.at[(16 - ROUTED) // 4, rest], other.at[(16 - ROUTED) // 4, rest]),
            (dense.at[whole], other.at[whole]),
            (s_v.at[1], s_other.at[0]),
            (s_v.at[3], s_other.at[1]),
        ]
        return [
            pltpu.make_async_remote_copy(
                src_ref=here,
                dst_ref=there,
                send_sem=gsend.at[i],
                recv_sem=grecv.at[i],
                device_id=(l, across),
                device_id_type=MESH,
            )
            for i, (here, there) in enumerate(pieces)
        ]

    at_turn = paired & (turn_left | turn_right)

    def route_copy(k, here):
        i = 15 - k
        piece = (i // 4, pl.ds(i % 4 * SPAN, SPAN))
        return pltpu.make_async_remote_copy(
            src_ref=here.at[piece],
            dst_ref=other.at[piece],
            send_sem=rsend.at[k],
            recv_sem=rrecv.at[k],
            device_id=(l, route_to),
            device_id_type=MESH,
        )

    def x_moves(q, dt):
        there, turn = (has_left, turn_left) if dt == -1 else (has_right, turn_right)
        return there & jnp.logical_not(paired & last & turn & (q == 3))

    def late_moves(q):
        return has_late & jnp.logical_not(at_turn & (lax.rem(q, 2) == 1))

    @pl.when(first & has_late)
    def _():
        late_copy(0, l).start()

    @pl.when(first)
    def _():
        early_copy(0, l).start()

    @pl.when(jnp.logical_not(first))
    def _():
        source_copy().start()

    @pl.when(at_turn)
    def _():
        for copy in turn_copies()[:1:-1]:
            copy.start()
        for k in range(ROUTED):
            route_copy(k, dense).start()
        for copy in turn_copies()[1::-1]:
            copy.start()

    @pl.when(on_route & jnp.logical_not(at_turn))
    def _():
        for k in range(ROUTED):
            route_copy(k, other).wait_recv()
            route_copy(k, other).start()

    def product(q, blocks, matrix, v, start):
        operand = jnp.concatenate([ext[q, where_is[p]] for p in blocks], axis=1)
        return jnp.dot(
            operand,
            matrix[v, start * 128 : (start + len(blocks)) * 128],
            preferred_element_type=F32,
        )

    def combine(total):
        re = total[0:16, 0:128] - total[16:32, 128:256]
        im = total[0:16, 128:256] + total[16:32, 0:128]
        return re, im

    def publish(q):
        for b in range(NB):
            for part in range(2):
                xo[q, b, part * 16 : part * 16 + 16] = xs[q + 1, part, b].astype(BF16)

        @pl.when(x_moves(q, -1))
        def _():
            x_copy(q, -1).start()

        @pl.when(x_moves(q, 1))
        def _():
            x_copy(q, 1).start()

        @pl.when((q == 0) & jnp.logical_not(first))
        def _():
            layer_copy(-1).start()

        @pl.when((q == 3) & jnp.logical_not(last))
        def _():
            layer_copy(1).start()

        for b in range(NB):
            for part in range(2):
                sol[q, part, pl.ds(b, 16, stride=4), :] = xs[q + 1, part, b]

    def others_late(q):
        for v in range(NB):
            other_acc[v] = product(q, [11 - c for c in places(v)[: 4 - v]], other, v, 0)

    def others_rest(q):
        for v in range(NB):
            other_acc[v] += product(q, [11 - c for c in places(v)[REMOTE:]], other, v, REMOTE)
        far_copy(q, 2, l).wait_recv()
        for v in range(NB):
            other_acc[v] += product(q, [11 - c for c in places(v)[4 - v : REMOTE]], other, v, 4 - v)

    def plane(q, carry):
        @pl.when(jnp.logical_not(first) & (q == 0))
        def _():
            own_copy().wait_recv()

        behind = at_turn & (lax.rem(q, 2) == 1)

        def begin(q):
            early_copy(q, l).wait_recv()
            for v in range(NB):
                acc[v] = product(q, [4 + c for c in places(v)[4 - v :]], dense, v, 4 - v)

        @pl.when(jnp.logical_not(behind))
        def _():
            begin(q)

        doubles = at_turn & (lax.rem(q, 2) == 0)

        @pl.when(doubles)
        def _():
            @pl.when(q == 0)
            def _():
                for copy in turn_copies():
                    copy.wait_recv()
                for k in range(ROUTED):
                    route_copy(k, dense).wait_recv()

            others_late(q)

        @pl.when((q == 3) & jnp.logical_not(last))
        def _():
            source_copy().wait_recv()

        def finish(v):
            b = row_of[v]
            re, im = combine(acc[v])
            ext[q + 1, OWN + b, 0:16] = (s_v[q + 1, 0, pl.ds(b, 16, stride=4), :] + re).astype(BF16)
            ext[q + 1, OWN + b, 16:32] = (s_v[q + 1, 1, pl.ds(b, 16, stride=4), :] + im).astype(BF16)
            xs[q + 1, 0, b] = re
            xs[q + 1, 1, b] = im

        @pl.when(late_moves(q))
        def _():
            late_copy(q, l).wait_recv()

        totals = [acc[v] + product(q, [4 + c for c in places(v)[: 4 - v]], dense, v, 0) for v in range(NB)]
        for v in range(NB):
            b = row_of[v]
            re, im = combine(totals[v])
            ext[q + 1, OWN + b, 0:16] = (s_v[q + 1, 0, pl.ds(b, 16, stride=4), :] + re).astype(BF16)
            ext[q + 1, OWN + b, 16:32] = (s_v[q + 1, 1, pl.ds(b, 16, stride=4), :] + im).astype(BF16)
            xs[q + 1, 0, b] = re
            xs[q + 1, 1, b] = im

        handing = (q == 3) & jnp.logical_not(last)
        onward = (q < 3) | jnp.logical_not(last)
        to = l + q // 3

        @pl.when((handing & has_late) | ((q < 3) & late_moves(q + 1)))
        def _():
            late_copy(q + 1, to).start()

        @pl.when(onward)
        def _():
            early_copy(q + 1, to).start()

        @pl.when(handing)
        def _():
            own_copy().start()

        sends_far = (handing & (l + 1 >= PAIRED)) | ((q == 1) & paired) | ((q == 2) & paired & last)

        @pl.when(sends_far & far_left & (w == 1))
        def _():
            far_copy(q + 1, -2, to).start()

        @pl.when(sends_far & far_right & (w == TURN - 2))
        def _():
            far_copy(q + 1, 2, to).start()

        @pl.when(doubles)
        def _():
            begin(q + 1)
            others_rest(q)
            into = jnp.where(turn_left, LEFT, RIGHT)
            for b in range(NB):
                re, im = combine(other_acc[3 - row_of[b]])
                there = [s_other[q // 2, part, pl.ds(b, 16, stride=4), :] for part in range(2)]
                ext[q + 1, into + b, 0:16] = (there[0] + re).astype(BF16)
                ext[q + 1, into + b, 16:32] = (there[1] + im).astype(BF16)

        @pl.when(jnp.logical_not(at_turn) | (lax.rem(q, 2) == 1))
        def _():
            publish(q)

        if q % 2 == 1:
            @pl.when(at_turn)
            def _():
                publish(q - 1)

        @pl.when(at_turn & last & (q == 3))
        def _():
            others_late(q)
            others_rest(q)
            for b in range(NB):
                re, im = combine(other_acc[3 - row_of[b]])
                xh[3, jnp.where(turn_left, 0, 1), b, 0:16] = re.astype(BF16)
                xh[3, jnp.where(turn_left, 0, 1), b, 16:32] = im.astype(BF16)

        return carry

    for q in range(4):
        plane(q, 0)

    load_w.wait()

    @pl.when(jnp.logical_not(first))
    def _():
        layer_copy(1).wait_recv()

    @pl.when(jnp.logical_not(last))
    def _():
        layer_copy(-1).wait_recv()

    for b in range(NB):
        for part in range(2):
            xs[0, part, b] = xlay[0, b, part * 16 : part * 16 + 16].astype(F32)
            xs[5, part, b] = xlay[1, b, part * 16 : part * 16 + 16].astype(F32)

    lane = lax.broadcasted_iota(jnp.int32, (16, 128), 1)

    def residual(q, carry):
        @pl.when(x_moves(q, -1))
        def _():
            x_copy(q, 1).wait_recv()

        @pl.when(x_moves(q, 1))
        def _():
            x_copy(q, -1).wait_recv()

        for b in range(NB):
            s_re = 6.0 - sh_v[q, pl.ds(b, 1), :]
            s_im = sh_v[q, pl.ds(4 + b, 1), :]
            x = [xs[q + 1, part, b] for part in range(2)]
            for part in range(2):
                up = pltpu.roll(x[part], 1, 1)
                before = pltpu.roll(xs[q + 1, part, b - 1], 1, 1) if b > 0 else jnp.zeros_like(up)
                down = pltpu.roll(x[part], 127, 1)
                after = pltpu.roll(xs[q + 1, part, b + 1], 127, 1) if b < 3 else jnp.zeros_like(up)
                beside = jnp.where(lane == 0, before, up) + jnp.where(lane == 127, after, down)
                beside = beside + xs[q, part, b] + xs[q + 2, part, b]
                half = slice(part * 16, part * 16 + 16)
                beside = beside + xh[q, 0, b, half].astype(F32) + xh[q, 1, b, half].astype(F32)
                cross = s_im * x[1] if part == 0 else -(s_im * x[0])
                value = s_re * x[part] + cross - beside
                res[q, part, pl.ds(b, 16, stride=4), :] = source(q, part, b) - value
        return carry

    for q in range(4):
        residual(q, 0)

    @pl.when(first & has_late)
    def _():
        late_copy(0, l).wait_send()

    @pl.when(first)
    def _():
        early_copy(0, l).wait_send()

    @pl.when(jnp.logical_not(first))
    def _():
        source_copy().wait_send()
        layer_copy(-1).wait_send()

    @pl.when(jnp.logical_not(last))
    def _():
        own_copy().wait_send()
        layer_copy(1).wait_send()

    @pl.when(at_turn)
    def _():
        for copy in turn_copies():
            copy.wait_send()

    @pl.when(on_route)
    def _():
        for k in range(ROUTED):
            route_copy(k, dense).wait_send()

    @pl.when(paired & (far_left & (w == 1) | far_right & (w == TURN - 2)))
    def _():
        far_copy(2, 2, l).wait_send()

        @pl.when(last)
        def _():
            far_copy(3, 2, l).wait_send()

    @pl.when(jnp.logical_not(last) & (l + 1 >= PAIRED) & (far_left & (w == 1) | far_right & (w == TURN - 2)))
    def _():
        far_copy(4, 2, l).wait_send()

    def drain(q, carry):
        @pl.when(x_moves(q, -1))
        def _():
            x_copy(q, -1).wait_send()

        @pl.when(x_moves(q, 1))
        def _():
            x_copy(q, 1).wait_send()

        handing = (q == 3) & jnp.logical_not(last)

        @pl.when((handing & has_late) | ((q < 3) & late_moves(q + 1)))
        def _():
            late_copy(q + 1, l).wait_send()

        @pl.when((q < 3) | handing)
        def _():
            early_copy(q + 1, l).wait_send()

        return carry

    lax.fori_loop(0, 4, drain, 0)


def write_results(sol, res, sol_out, res_out, sem):
    copies = [
        pltpu.make_async_copy(here.at[q], there.at[q], sem.at[i, q])
        for q in range(4)
        for i, (here, there) in enumerate(((sol, sol_out), (res, res_out)))
    ]
    for copy in copies:
        copy.start()
    for copy in copies:
        copy.wait()


def per_device(layers, tiles, source_field, wave_shift, frontal_blocks, block_columns):
    field = pltpu.VMEM((4, 2, 64, 128), F32)
    hbm = pl.BlockSpec(memory_space=pltpu.HBM)
    dma = pltpu.SemaphoreType.DMA
    sol, res = pl.pallas_call(
        functools.partial(kernel, layers, tiles),
        out_shape=(field, field),
        in_specs=[hbm, hbm, hbm, hbm],
        out_specs=(pl.BlockSpec(memory_space=pltpu.VMEM),) * 2,
        scratch_shapes=[
            pltpu.VMEM((5, 2, 64, 128), F32),
            pltpu.VMEM((4, 8, 128), F32),
            pltpu.VMEM((4, 8, 2, 128, 128), BF16),
            pltpu.SMEM((4, 8), jnp.int32),
            pltpu.VMEM((4, 1152, 256), BF16),
            pltpu.VMEM((4, 1152, 256), BF16),
            pltpu.VMEM((2, 2, 64, 128), F32),
            pltpu.VMEM((5, 20, 32, 128), BF16),
            pltpu.VMEM((4, 4, 32, 128), BF16),
            pltpu.VMEM((4, 2, 4, 32, 128), BF16),
            pltpu.VMEM((2, 4, 32, 128), BF16),
            pltpu.VMEM((6, 2, 4, 16, 128), F32),
            pltpu.VMEM((4, 32, 256), F32),
            pltpu.VMEM((4, 32, 256), F32),
            dma((7,)),
            dma((5,)),
            dma((4,)),
            dma((5,)),
            dma((4,)),
            dma((5,)),
            dma((4,)),
            dma((4, 2)),
            dma((4, 2)),
            dma((4,)),
            dma((4,)),
            dma((4,)),
            dma((4,)),
            dma((ROUTED,)),
            dma((ROUTED,)),
        ],
        compiler_params=pltpu.CompilerParams(
            collective_id=0, has_side_effects=True, vmem_limit_bytes=32 * 1024 * 1024
        ),
    )(
        *[
            pltpu.with_memory_space_constraint(operand, pltpu.HBM)
            for operand in (
                source_field.reshape(4, 2, 64, 128),
                wave_shift.reshape(4, 8, 128),
                frontal_blocks[0],
                block_columns[0],
            )
        ]
    )
    whole = jax.ShapeDtypeStruct((4, 2, 64, 128), F32)
    out = pl.BlockSpec(memory_space=pltpu.HBM)
    sol, res = pl.pallas_call(
        write_results,
        out_shape=(whole, whole),
        in_specs=[pl.BlockSpec(memory_space=pltpu.VMEM)] * 2,
        out_specs=(out, out),
        scratch_shapes=[dma((2, 4))],
        compiler_params=pltpu.CompilerParams(vmem_limit_bytes=8 * 1024 * 1024),
    )(*[pltpu.with_memory_space_constraint(result, pltpu.VMEM) for result in (sol, res)])
    return sol.reshape(4, 2, 16, 1, 512), res.reshape(4, 2, 16, 1, 512)


def solution(mesh):
    placed = (
        P("layer", None, None, "tile", None),
        P("layer", None, "tile", None),
        P("layer", "tile", None, None, None, None),
        P("layer", "tile", None),
    )
    return jax.shard_map(
        functools.partial(per_device, mesh.shape["layer"], mesh.shape["tile"]),
        mesh=mesh,
        in_specs=placed,
        out_specs=(P("layer", None, None, "tile", None), P("layer", None, None, "tile", None)),
        check_vma=False,
    )
```
